32 devices in a mesh: row: 4 (over y, core), col: 8 (over z, x).
Axes of the slice: x: 2, y: 2, z: 4, core: 2. Of those that a mesh axis runs over, the one named last changes fastest.
Arguments:
- density: float32 [4, 8, 7, 2, 128, 128], P('row', 'col'), may hold values from -1 to 2, as said below
- hamiltonian: float32 [4, 8, 7, 2, 128, 128], P('row', 'col'), may hold values from -2 to 4, as said below
- offsets: int32 [7, 3], replicated, may hold values from -1 to 1, as said below
- branch: int32 [3], replicated, may hold values from 0 to 1, as said below
Outputs:
- new_density: float32 [4, 8, 7, 2, 128, 128], P('row', 'col')
- grad_density: float32 [4, 8, 7, 2, 128, 128], P('row', 'col')
- totals: float32 [2], replicated
The draws below stay inside these ranges and needn't reach their ends.
Inputs may be any that keep to these rules, and one draw needn't show every extreme that they name: 7 distinct offsets; (0, 0, 0) is one of them and with each offset its negative (layer step modulo 2) is another; row and column steps lie in -1 to 1, and nonzero row steps and nonzero column steps both occur. `branch`: each entry is 0 or 1, and not all entries are equal. `density`: the matrix is symmetric: entry [p, q, t, s] is the transpose of the entry of the opposite offset at the transposed block position. `hamiltonian`: the matrix is symmetric, in the same sense as the density.
All inputs are finite; a program needn't handle non-finite values.
Results may differ from the reference program's by a relative error of at most 0.0003.
Values sent between devices are 32-bit elements; how exact they have to be, the bound alone decides.
No kernel may reach another device: no remote copies, remote signals or barrier semaphores. Data moves between devices by JAX's collectives and lax.ppermute only.
A program may use at most 128 MiB of HBM per device.

```python
import jax
import jax.numpy as jnp
from jax import lax

BLOCK = 128
LAYERS = 2
SLOTS = 7
STEPS = 3
ORDER = 8192
N_ROW = 4
N_COL = 8


def offset_table(key):
    candidates = jnp.array([[1, -1, 0], [1, -1, 1], [1, 0, 0], [1, 0, 1], [1, 1, 0], [1, 1, 1], [0, 1, 0], [0, 1, 1]], jnp.int32)
    picked = jax.random.permutation(jax.random.fold_in(key, 11), 8)
    chosen = candidates[picked[:3]]
    negated = jnp.stack([-chosen[:, 0], -chosen[:, 1], (LAYERS - chosen[:, 2]) % LAYERS], axis=1)
    offset_rows = jnp.concatenate([jnp.zeros((1, 3), jnp.int32), chosen, negated], axis=0)
    shuffle = jax.random.permutation(jax.random.fold_in(key, 12), SLOTS)
    return offset_rows[shuffle]


def zero_mask(key):
    return jnp.all(offset_table(key) == 0, axis=1).astype(jnp.float32)


def draw_offsets(key, part):
    return offset_table(key)


def draw_branch(key, part):
    number = jax.random.randint(jax.random.fold_in(key, 41), (), 1, 2 ** STEPS - 1, jnp.int32)
    powers = 2 ** jnp.arange(STEPS, dtype=jnp.int32)
    return (number // powers % 2).astype(jnp.int32)


def symmetric(raw_blocks, table):
    negated = jnp.stack([-table[:, 0], -table[:, 1], (LAYERS - table[:, 2]) % LAYERS], axis=1)
    matching = jnp.all(negated[:, None, :] == table[None, :, :], axis=-1).astype(jnp.int32)
    opposite = jnp.argmax(matching, axis=1).astype(jnp.int32)
    mirrored_list = []
    for slot in range(SLOTS):
        other = jnp.take(raw_blocks, opposite[slot], axis=2)
        other = jnp.roll(other, -table[slot, 0], axis=0)
        other = jnp.roll(other, table[slot, 1], axis=1)
        other = jnp.roll(other, -table[slot, 2], axis=2)
        mirrored_list.append(jnp.swapaxes(other, -1, -2))
    mirrored = jnp.stack(mirrored_list, axis=2)
    return (raw_blocks + mirrored) * 0.5 ** 0.5


def rough_part(noise_key, shape):
    return jax.random.truncated_normal(noise_key, -4.0, 4.0, shape, jnp.float32)


def draw_density(key, part):
    shape = (N_ROW, N_COL, SLOTS, LAYERS, BLOCK, BLOCK)
    table = offset_table(key)
    zero_slot = zero_mask(key)
    noise_key = jax.random.fold_in(key, 21)
    rough_key = jax.random.fold_in(key, 23)
    noise_part = symmetric(rough_part(noise_key, shape), table) * (0.5 / (BLOCK * SLOTS) ** 0.5)
    levels = 0.25 + 0.5 * lax.iota(jnp.float32, N_ROW) / (N_ROW - 1)
    roughness = jax.random.uniform(rough_key, (N_ROW, N_COL, SLOTS, LAYERS, BLOCK), jnp.float32, 0.6, 1.4)
    diagonal_part = levels[:, None, None, None, None] * roughness * zero_slot[None, None, :, None, None]
    unit_block = jnp.eye(BLOCK, dtype=jnp.float32)
    return noise_part + diagonal_part[..., None] * unit_block


def draw_hamiltonian(key, part):
    shape = (N_ROW, N_COL, SLOTS, LAYERS, BLOCK, BLOCK)
    table = offset_table(key)
    zero_slot = zero_mask(key)
    noise_key = jax.random.fold_in(key, 31)
    onsite_key = jax.random.fold_in(key, 33)
    hopping = symmetric(rough_part(noise_key, shape), table) * 0.3
    onsite = jax.random.uniform(onsite_key, (N_ROW, N_COL, SLOTS, LAYERS, BLOCK), jnp.float32, 0.5, 2.0)
    onsite = onsite * zero_slot[None, None, :, None, None]
    unit_block = jnp.eye(BLOCK, dtype=jnp.float32)
    return hopping + onsite[..., None] * unit_block


def setup_inputs(seed: int = 0) -> dict:
    key_of = jax.random.split(jax.random.key(seed), 5)
    density = draw_density(jax.random.fold_in(key_of[4], 71), 0)
    hamiltonian = draw_hamiltonian(jax.random.fold_in(key_of[4], 71), 0)
    offsets = draw_offsets(jax.random.fold_in(key_of[4], 71), 0)
    branch = draw_branch(jax.random.fold_in(key_of[4], 71), 0)
    return dict(density=density, hamiltonian=hamiltonian, offsets=offsets, branch=branch)


FULL_PRECISION = lax.Precision.HIGHEST


def pair_tables(offsets, row_count, col_count, layer_count):
    moduli = jnp.array([row_count, col_count, layer_count], jnp.int32)
    summed = offsets[:, None, :] + offsets[None, :, :]
    differ = summed[None, :, :, :] - offsets[:, None, None, :]
    matches = jnp.all(differ % moduli == 0, axis=-1).astype(jnp.int32)
    partner = jnp.argmax(matches, axis=2).astype(jnp.int32)
    usable = jnp.max(matches, axis=2)
    return partner, usable


def sparse_product(left, right, offsets, partner, usable):
    count_offsets = offsets.shape[0]

    def pair_step(pair_index, running):
        target = (pair_index // count_offsets).astype(jnp.int32)
        left_index = (pair_index % count_offsets).astype(jnp.int32)
        partner_slot = partner[target, left_index]
        left_part = lax.dynamic_index_in_dim(left, left_index, 2, keepdims=False)
        left_part = jnp.roll(left_part, offsets[partner_slot, 1], axis=1)
        right_part = lax.dynamic_index_in_dim(right, partner_slot, 2, keepdims=False)
        right_part = jnp.roll(right_part, -offsets[left_index, 0], axis=0)
        right_part = jnp.roll(right_part, -offsets[left_index, 2], axis=2)
        block_term = jnp.einsum('pqsab,pqsbc->pqsac', left_part, right_part, precision=FULL_PRECISION)
        keep_mask = usable[target, left_index].astype(block_term.dtype)
        current = lax.dynamic_index_in_dim(running, target, 2, keepdims=False)
        return lax.dynamic_update_index_in_dim(running, current + keep_mask * block_term, target, 2)

    return lax.fori_loop(0, count_offsets * count_offsets, pair_step, jnp.zeros_like(left))


def reference(density, hamiltonian, offsets, branch):
    partner, usable = pair_tables(offsets, N_ROW, N_COL, LAYERS)
    zero_slot = jnp.all(offsets == 0, axis=1).astype(jnp.float32)
    identity_part = zero_slot[:, None, None, None] * jnp.eye(BLOCK, dtype=jnp.float32)
    branch_signs = (2 * branch - 1).astype(jnp.float32)
    iterates = [density]
    for step in range(STEPS):
        current = iterates[-1]
        square = sparse_product(current, current, offsets, partner, usable)
        iterates.append(current + branch_signs[step] * (current - square))
    new_density = iterates[-1]
    energy = jnp.sum(hamiltonian * new_density) / ORDER
    occupation = jnp.sum(new_density * identity_part) / ORDER
    totals = jnp.stack([energy, occupation])
    outer_grad = hamiltonian + (occupation - 0.5) * identity_part
    for step in range(STEPS - 1, -1, -1):
        current = iterates[step]
        cross = sparse_product(outer_grad, current, offsets, partner, usable) + sparse_product(current, outer_grad, offsets, partner, usable)
        outer_grad = (1.0 + branch_signs[step]) * outer_grad - branch_signs[step] * cross
    return (new_density, outer_grad, totals)
```

```python
import functools

import jax
import jax.numpy as jnp
from jax import lax
from jax.experimental import pallas as pl
from jax.experimental.pallas import tpu as pltpu
from jax.sharding import PartitionSpec as P

F32 = jnp.float32
BF16 = jnp.bfloat16
EXTRA = 8


def iotas(size):
    shape = (size, size)
    return lax.broadcasted_iota(jnp.int32, shape, 0), lax.broadcasted_iota(jnp.int32, shape, 1)


def store_split(dst, index, value):
    size = value.shape[-1]
    high = value.astype(BF16)
    dst[index + (slice(None), slice(0, size))] = high
    dst[index + (slice(None), slice(size, 2 * size))] = (value - high.astype(F32)).astype(BF16)


def quadrants(q):
    size = q.shape[-1] // 2
    return (q[:size, :size] + q[size:, size:]) + (q[:size, size:] + q[size:, :size])


def pack_pair(first, second):
    size = first.shape[-1]
    row, col = iotas(size)
    body = jnp.where(row <= col, first, second)
    diagonal = jnp.sum(jnp.where(row == col, second, 0.0), axis=0, keepdims=True)
    return jnp.concatenate([body, jnp.broadcast_to(diagonal, (EXTRA, size))], axis=0)


def unpack_pair(packed):
    size = packed.shape[-1]
    row, col = iotas(size)
    body = packed[:size]
    turned = body.T
    second_diagonal = packed[size : size + 1]
    first = jnp.where(row <= col, body, turned)
    second = jnp.where(row > col, body, jnp.where(row == col, second_diagonal, turned))
    return first, second


def slot_offsets(off, t, layers):
    return off[t, 0], off[t, 1], lax.rem(off[t, 2] + layers, layers)


def zero_slot(off, slots):
    z = jnp.int32(0)
    for t in range(slots):
        hit = (off[t, 0] == 0) & (off[t, 1] == 0) & (off[t, 2] == 0)
        z = jnp.where(hit, jnp.int32(t), z)
    return z


def sign_of(branch, k):
    return (2 * branch[k] - 1).astype(F32)


def vertex_sums(off, left, right, acc, keep):
    slots, layers = left.shape[0], left.shape[1]
    acc[...] = jnp.zeros_like(acc)
    for t in range(slots):
        r, _, l = slot_offsets(off, t, layers)

        def add(t=t, r=r, l=l):
            for s in range(layers):
                q = lax.dot_general(
                    left[t, s], right[t, s], (((0,), (0,)), ((), ())), preferred_element_type=F32
                )
                acc[r + 1, lax.rem(s + l, layers)] += quadrants(q)

        if keep is None:
            add()
        else:
            pl.when(keep(r))(add)


def symmetric(value):
    return value + value.T


def edge_product(lefts, rights):
    size = lefts[0].shape[0]
    high = [x[:, :size] for x in lefts]
    low = [x[:, size:] for x in lefts]
    lhs = jnp.concatenate([jnp.concatenate(high, 1), jnp.concatenate(low, 1)], 0)
    rhs = jnp.concatenate(rights, 0)
    return quadrants(jnp.dot(lhs, rhs, preferred_element_type=F32))


def fill_neighbours(dst, own, low, high, which):
    for k in range(dst.shape[1] // 2):
        for slot, message in ((0, low), (2, high)):
            first, second = unpack_pair(message[which, k])
            store_split(dst, (slot, 2 * k), first)
            store_split(dst, (slot, 2 * k + 1), second)
    for s in range(dst.shape[1]):
        store_split(dst, (1, s), own[s])


def add_sums(value, low, high, which):
    out = list(value)
    for k in range(len(out) // 2):
        for message in (low, high):
            first, second = unpack_pair(message[which, k])
            out[2 * k] = out[2 * k] + first
            out[2 * k + 1] = out[2 * k + 1] + second
    return out


def put_pairs(ref, which, blocks):
    for k in range(len(blocks) // 2):
        ref[which, k] = pack_pair(blocks[2 * k], blocks[2 * k + 1])


def split_all(src, dst):
    for t in range(src.shape[0]):
        for s in range(src.shape[1]):
            store_split(dst, (t, s), src[t, s])


def send_sums(acc, which, up, down, sym):
    layers = acc.shape[1]
    for r, ref in ((2, up), (0, down)):
        blocks = [acc[r, s] for s in range(layers)]
        put_pairs(ref, which, [symmetric(b) for b in blocks] if sym else blocks)


def start_kernel(off, x, h, up, down, side, x_local, xs, acc):
    slots, layers = x.shape[0], x.shape[1]
    z = zero_slot(off, slots)
    split_all(x, xs)
    vertex_sums(off, xs, xs, acc, None)
    diag = [x[z, s] for s in range(layers)]
    diag_h = [h[z, s] for s in range(layers)]
    for ref in (up, down, side):
        put_pairs(ref, 0, diag)
        put_pairs(ref, 1, diag_h)
    send_sums(acc, 2, up, down, False)
    for s in range(layers):
        x_local[s] = acc[1, s]


def square_step(off, s_k, x, x_local, row_low, row_high, col_low, col_high, new, xs, rows, cols, sums_at):
    slots, layers = x.shape[0], x.shape[1]
    z = zero_slot(off, slots)
    split_all(x, xs)
    own = [x[z, s] for s in range(layers)]
    fill_neighbours(rows, own, row_low, row_high, 0)
    fill_neighbours(cols, own, col_low, col_high, 0)
    square = add_sums([x_local[s] for s in range(layers)], row_low, row_high, sums_at)
    for s in range(layers):
        new[z, s] = own[s] + s_k * (own[s] - square[s])
    for i in range(slots - 1):
        t = i + (i >= z).astype(jnp.int32)
        r, c, l = slot_offsets(off, t, layers)
        for s in range(layers):
            e = xs[t, s]
            product = edge_product([cols[1 - c, s], e], [e, rows[1 + r, lax.rem(s + l, layers)]])
            e32 = x[t, s]
            new[t, s] = e32 + s_k * (e32 - product)
    return z


def square_kernel(k, sums_at, off, branch, x, x_local, row_low, row_high, col_low, col_high,
                  new, up, down, side, new_local, xs, ns, rows, cols, acc):
    layers = x.shape[1]
    z = square_step(off, sign_of(branch, k), x, x_local, row_low, row_high, col_low, col_high,
                    new, xs, rows, cols, sums_at)
    diag = [new[z, s] for s in range(layers)]
    for ref in (up, down, side):
        put_pairs(ref, 0, diag)
    split_all(new, ns)
    vertex_sums(off, ns, ns, acc, None)
    send_sums(acc, 1, up, down, False)
    for s in range(layers):
        new_local[s] = acc[1, s]


def last_square_kernel(k, sums_at, off, branch, x, x_local, row_low, row_high, col_low, col_high, h,
                       new, sums, xs, rows, cols):
    slots, layers, size = x.shape[0], x.shape[1], x.shape[2]
    z = square_step(off, sign_of(branch, k), x, x_local, row_low, row_high, col_low, col_high,
                    new, xs, rows, cols, sums_at)
    energy = jnp.zeros((size, size), F32)
    for t in range(slots):
        for s in range(layers):
            energy = energy + h[t, s] * new[t, s]
    row, col = iotas(size)
    trace = jnp.zeros((size, size), F32)
    for s in range(layers):
        trace = trace + jnp.where(row == col, new[z, s], 0.0)
    sums[0:1, :] = jnp.broadcast_to(jnp.sum(energy, keepdims=True), (1, size))
    sums[1:2, :] = jnp.broadcast_to(jnp.sum(trace, keepdims=True), (1, size))
    sums[2:, :] = jnp.zeros_like(sums[2:, :])


def turn_square_kernel(k, off, branch, x, x_local, row_low, row_high, col_low, col_high, h,
                       new, up, down, side, new_local, h_local, cross_local,
                       xs, hs, news, rows, cols, acc):
    slots, layers = x.shape[0], x.shape[1]
    z = square_step(off, sign_of(branch, k), x, x_local, row_low, row_high, col_low, col_high,
                    new, xs, rows, cols, 1)
    diag = [new[z, s] for s in range(layers)]
    for ref in (up, down, side):
        put_pairs(ref, 0, diag)
    split_all(new, news)
    split_all(h, hs)
    vertex_sums(off, news, news, acc, None)
    send_sums(acc, 1, up, down, False)
    for s in range(layers):
        new_local[s] = acc[1, s]
    vertex_sums(off, hs, news, acc, None)
    send_sums(acc, 2, up, down, True)
    for s in range(layers):
        h_local[s] = symmetric(acc[1, s])
    vertex_sums(off, news, xs, acc, None)
    send_sums(acc, 3, up, down, True)
    for s in range(layers):
        cross_local[s] = symmetric(acc[1, s])


def gradient_edges(off, s_k, g, new, gs, xs, g_rows, g_cols, x_rows, x_cols, z):
    slots, layers = g.shape[0], g.shape[1]
    for i in range(slots - 1):
        t = i + (i >= z).astype(jnp.int32)
        r, c, l = slot_offsets(off, t, layers)
        for s in range(layers):
            e, f = gs[t, s], xs[t, s]
            b = lax.rem(s + l, layers)
            product = edge_product(
                [g_cols[1 - c, s], x_cols[1 - c, s], e, f], [f, e, x_rows[1 + r, b], g_rows[1 + r, b]]
            )
            new[t, s] = (1.0 + s_k) * g[t, s] - s_k * product


def first_gradient_kernel(k, off, branch, h, x, x_before, h_local, h_row_low, h_row_high, h_col_low, h_col_high,
                          row_low, row_high, col_low, col_high,
                          new, up, down, side, new_local,
                          gs, xs, ns, bs, g_rows, g_cols, x_rows, x_cols, acc):
    layers = x.shape[1]
    s_k = sign_of(branch, k)
    z = zero_slot(off, x.shape[0])
    split_all(h, gs)
    split_all(x, xs)
    own_h = [h[z, s] for s in range(layers)]
    own_x = [x[z, s] for s in range(layers)]
    fill_neighbours(g_rows, own_h, h_row_low, h_row_high, 1)
    fill_neighbours(g_cols, own_h, h_col_low, h_col_high, 1)
    fill_neighbours(x_rows, own_x, row_low, row_high, 0)
    fill_neighbours(x_cols, own_x, col_low, col_high, 0)
    cross = add_sums([h_local[s] for s in range(layers)], row_low, row_high, 2)
    for s in range(layers):
        new[z, s] = (1.0 + s_k) * own_h[s] - s_k * cross[s]
    gradient_edges(off, s_k, h, new, gs, xs, g_rows, g_cols, x_rows, x_cols, z)
    diag = [new[z, s] for s in range(layers)]
    for ref in (up, down, side):
        put_pairs(ref, 0, diag)
    split_all(new, ns)
    split_all(x_before, bs)
    vertex_sums(off, ns, bs, acc, None)
    send_sums(acc, 1, up, down, True)
    for s in range(layers):
        new_local[s] = symmetric(acc[1, s])


def next_gradient_kernel(k, order, off, branch, sums, gh, x_after, x, x_before, gh_local, cross_local,
                         g_row_low, g_row_high, g_col_low, g_col_high,
                         after_row_low, after_row_high, after_col_low, after_col_high,
                         row_low, row_high, col_low, col_high,
                         new, up, down, side, new_local,
                         g, gs, xs, ns, bs, g_rows, g_cols, x_rows, x_cols, acc):
    slots, layers, size = x.shape[0], x.shape[1], x.shape[2]
    s_k = sign_of(branch, k)
    s_after = sign_of(branch, k + 1)
    excess = sums[1:2, :] * (1.0 / order) - 0.5
    z = zero_slot(off, slots)
    row, col = iotas(size)
    eye = jnp.where(row == col, excess * (1.0 + s_after), 0.0)
    scale = excess * (-2.0 * s_after)
    for t in range(slots):
        for s in range(layers):
            g[t, s] = gh[t, s] + scale * x_after[t, s]
    for s in range(layers):
        g[z, s] = g[z, s] + eye
    split_all(g, gs)
    split_all(x, xs)
    own_g = [g[z, s] for s in range(layers)]
    own_x = [x[z, s] for s in range(layers)]
    for dst, pairs in (
        (g_rows, ((0, g_row_low, after_row_low), (2, g_row_high, after_row_high))),
        (g_cols, ((0, g_col_low, after_col_low), (2, g_col_high, after_col_high))),
    ):
        for slot, message, after in pairs:
            for j in range(layers // 2):
                blocks = unpack_pair(message[0, j])
                befores = unpack_pair(after[0, j])
                for p in range(2):
                    store_split(dst, (slot, 2 * j + p), blocks[p] + scale * befores[p] + eye)
        for s in range(layers):
            store_split(dst, (1, s), own_g[s])
    fill_neighbours(x_rows, own_x, row_low, row_high, 0)
    fill_neighbours(x_cols, own_x, col_low, col_high, 0)
    own_sums = add_sums([gh_local[s] for s in range(layers)], g_row_low, g_row_high, 1)
    cross_sums = add_sums([cross_local[s] for s in range(layers)], after_row_low, after_row_high, 3)
    twice = 2.0 * (1.0 + s_after) * excess
    for s in range(layers):
        cross = own_sums[s] + scale * cross_sums[s] + twice * own_x[s]
        new[z, s] = (1.0 + s_k) * own_g[s] - s_k * cross
    gradient_edges(off, s_k, g, new, gs, xs, g_rows, g_cols, x_rows, x_cols, z)
    diag = [new[z, s] for s in range(layers)]
    for ref in (up, down, side):
        put_pairs(ref, 0, diag)
    split_all(new, ns)
    split_all(x_before, bs)
    vertex_sums(off, ns, bs, acc, None)
    send_sums(acc, 1, up, down, True)
    for s in range(layers):
        new_local[s] = symmetric(acc[1, s])


def last_gradient_kernel(k, off, branch, g, x, g_local, g_row_low, g_row_high, g_col_low, g_col_high,
                         row_low, row_high, col_low, col_high,
                         new, gs, xs, g_rows, g_cols, x_rows, x_cols):
    layers = x.shape[1]
    s_k = sign_of(branch, k)
    z = zero_slot(off, x.shape[0])
    split_all(g, gs)
    split_all(x, xs)
    own_g = [g[z, s] for s in range(layers)]
    own_x = [x[z, s] for s in range(layers)]
    fill_neighbours(g_rows, own_g, g_row_low, g_row_high, 0)
    fill_neighbours(g_cols, own_g, g_col_low, g_col_high, 0)
    fill_neighbours(x_rows, own_x, row_low, row_high, 0)
    fill_neighbours(x_cols, own_x, col_low, col_high, 0)
    cross = add_sums([g_local[s] for s in range(layers)], g_row_low, g_row_high, 1)
    for s in range(layers):
        new[z, s] = (1.0 + s_k) * own_g[s] - s_k * cross[s]
    gradient_edges(off, s_k, g, new, gs, xs, g_rows, g_cols, x_rows, x_cols, z)


def call(kernel, smem, vmem, outs, scratch):
    return pl.pallas_call(
        kernel,
        out_shape=[jax.ShapeDtypeStruct(shape, F32) for shape in outs],
        in_specs=[pl.BlockSpec(memory_space=pltpu.SMEM)] * len(smem)
        + [pl.BlockSpec(memory_space=pltpu.VMEM)] * len(vmem),
        out_specs=[pl.BlockSpec(memory_space=pltpu.VMEM)] * len(outs),
        scratch_shapes=scratch,
        compiler_params=pltpu.CompilerParams(vmem_limit_bytes=40 * 1024 * 1024),
    )(*smem, *vmem)


def ring(axis):
    count = lax.axis_size(axis)
    forward = [(i, (i + 1) % count) for i in range(count)]
    return forward, [(b, a) for a, b in forward]


def exchange(up, down, side):
    row_forward, row_backward = ring("row")
    col_forward, col_backward = ring("col")
    return (
        lax.ppermute(up, "row", row_forward),
        lax.ppermute(down, "row", row_backward),
        lax.ppermute(side, "col", col_forward),
        lax.ppermute(side, "col", col_backward),
    )


def total_over(value, axis):
    count = lax.axis_size(axis)
    if count & (count - 1):
        return lax.psum(value, axis)
    step = 1
    while step < count:
        value = value + lax.ppermute(value, axis, [(i, i ^ step) for i in range(count)])
        step *= 2
    return value


def sparse_path(density, hamiltonian, offsets, branch):
    slots, layers, size = density.shape[2:5]
    full = (slots, layers, size, size)
    x0 = density.reshape(full)
    h = hamiltonian.reshape(full)
    order = size * layers * lax.axis_size("row") * lax.axis_size("col")
    pairs = layers // 2

    def message(n):
        return (n, pairs, size + EXTRA, size)

    local = (layers, size, size)
    split = pltpu.VMEM((slots, layers, size, 2 * size), BF16)
    three = pltpu.VMEM((3, layers, size, 2 * size), BF16)
    acc = pltpu.VMEM((3, layers, size, size), F32)
    smem = (offsets, branch)
    up, down, side, local0 = call(
        start_kernel, (offsets,), (x0, h), [message(3), message(3), message(2), local], [split, acc]
    )
    near0 = exchange(up, down, side)
    x1, up, down, side, local1 = call(
        functools.partial(square_kernel, 0, 2), smem, (x0, local0, *near0),
        [full, message(2), message(2), message(1), local], [split, split, three, three, acc],
    )
    near1 = exchange(up, down, side)
    x2, up, down, side, local2, h_local, cross_local = call(
        functools.partial(turn_square_kernel, 1), smem, (x1, local1, *near1, h),
        [full, message(4), message(4), message(1), local, local, local],
        [split, split, split, three, three, acc],
    )
    near2 = exchange(up, down, side)
    gh, up, down, side, gh_local = call(
        functools.partial(first_gradient_kernel, 2), smem, (h, x2, x1, h_local, *near0, *near2),
        [full, message(2), message(2), message(1), local],
        [split, split, split, split, three, three, three, three, acc],
    )
    near_gh = exchange(up, down, side)
    x3, sums = call(
        functools.partial(last_square_kernel, 2, 1), smem, (x2, local2, *near2, h),
        [full, (8, size)], [split, three, three],
    )
    sums = total_over(total_over(sums, "row"), "col")
    g1, up, down, side, g1_local = call(
        functools.partial(next_gradient_kernel, 1, float(order)), smem,
        (sums, gh, x2, x1, x0, gh_local, cross_local, *near_gh, *near2, *near1),
        [full, message(2), message(2), message(1), local],
        [pltpu.VMEM(full, F32), split, split, split, split, three, three, three, three, acc],
    )
    near_g1 = exchange(up, down, side)
    (g0,) = call(
        functools.partial(last_gradient_kernel, 0), smem, (g1, x0, g1_local, *near_g1, *near0),
        [full], [split, split, three, three, three, three],
    )
    totals = sums[:2, 0] / order
    return x3.reshape(density.shape), g0.reshape(density.shape), totals


FULL_PRECISION = lax.Precision.HIGHEST


def with_halo(block, sides, width):
    for axis, dim in sides:
        count = lax.axis_size(axis)
        forward = [(i, i + 1) for i in range(count - 1)]
        forward.append((count - 1, 0))
        backward = [(target, source) for source, target in forward]
        low = lax.ppermute(
            lax.slice_in_dim(block, block.shape[dim] - width, None, axis=dim), axis, forward
        )
        high = lax.ppermute(lax.slice_in_dim(block, 0, width, axis=dim), axis, backward)
        block = jnp.concatenate([low, block, high], axis=dim)
    return block


def pair_tables(offsets, row_count, col_count, layer_count):
    moduli = jnp.array([row_count, col_count, layer_count], jnp.int32)
    summed = offsets[:, None, :] + offsets[None, :, :]
    differ = summed[None, :, :, :] - offsets[:, None, None, :]
    matches = jnp.all(differ % moduli == 0, axis=-1).astype(jnp.int32)
    partner = jnp.argmax(matches, axis=2)
    usable = jnp.max(matches, axis=2)
    return (partner, usable)


def sparse_product(left_rim, right_rim, offsets, partner, usable):
    count_offsets = offsets.shape[0]
    layer_count = left_rim.shape[2]
    col_pick = 1 - offsets[:, 1]
    row_pick = 1 + offsets[:, 0]
    layer_pick = (jnp.arange(layer_count, dtype=jnp.int32)[None, :] + offsets[:, 2:3]) % layer_count
    left_slots = jnp.arange(count_offsets, dtype=jnp.int32)

    def one_target(target):
        partners_row = partner[target]
        keep_mask = usable[target].astype(jnp.float32)
        left_part = left_rim[col_pick[partners_row], left_slots] * keep_mask[:, None, None, None]
        right_part = right_rim[row_pick[:, None], partners_row[:, None], layer_pick]
        return jnp.einsum("tsab,tsbc->sac", left_part, right_part, precision=FULL_PRECISION)

    return lax.map(one_target, jnp.arange(count_offsets, dtype=jnp.int32))


def iterate_rims(field):
    rows_rim = with_halo(field, (("row", 0),), 1)[:, 0]
    cols_rim = with_halo(field, (("col", 1),), 1)[0]
    return (cols_rim, rows_rim)


def outer_rims(field):
    rows_rim = with_halo(field, (("row", 0),), 1)[:, 0]
    cols_rim = with_halo(field, (("col", 1),), 1)[0]
    return (cols_rim, rows_rim)


def general_path(density, hamiltonian, offsets, branch):
    row_count = lax.axis_size("row")
    col_count = lax.axis_size("col")
    step_count = branch.shape[0]
    layer_count = density.shape[3]
    block_size = density.shape[4]
    matrix_order = block_size * layer_count * row_count * col_count
    partner, usable = pair_tables(offsets, row_count, col_count, layer_count)
    zero_slot = jnp.all(offsets == 0, axis=1).astype(jnp.float32)
    identity_part = zero_slot[:, None, None, None] * jnp.eye(block_size, dtype=jnp.float32)
    branch_signs = (2 * branch - 1).astype(jnp.float32)
    density_rows = with_halo(density, (("row", 0),), 1)[:, 0]
    density_cols = with_halo(density, (("col", 1),), 1)[0]
    density_rims = (density_cols, density_rows)
    iterates = [density]
    rims = [density_rims]
    for step in range(step_count):
        current = iterates[-1]
        square = sparse_product(rims[-1][0], rims[-1][1], offsets, partner, usable)[None, None]
        following = current + branch_signs[step] * (current - square)
        iterates.append(following)
        if step + 1 < step_count:
            rims.append(iterate_rims(following))
    new_density = iterates[-1]
    global_sums = lax.psum(
        (jnp.sum(hamiltonian * new_density), jnp.sum(new_density * identity_part)), ("row", "col")
    )
    totals = jnp.stack(global_sums) / matrix_order
    excess = totals[1] - 0.5
    outer_grad = hamiltonian + excess * identity_part
    last = step_count - 1
    last_cols, last_rows = rims[last]
    cotangent_rows = with_halo(outer_grad, (("row", 0),), 1)[:, 0]
    cotangent_cols = with_halo(outer_grad, (("col", 1),), 1)[0]
    cross_terms = sparse_product(
        cotangent_cols, last_rows, offsets, partner, usable
    ) + sparse_product(last_cols, cotangent_rows, offsets, partner, usable)
    cross_terms = cross_terms[None, None]
    outer_grad = (1.0 + branch_signs[last]) * outer_grad - branch_signs[last] * cross_terms
    for step in range(last - 1, -1, -1):
        grad_cols, grad_rows = outer_rims(outer_grad)
        step_cols, step_rows = rims[step]
        cross_terms = sparse_product(
            grad_cols, step_rows, offsets, partner, usable
        ) + sparse_product(step_cols, grad_rows, offsets, partner, usable)
        outer_grad = (1.0 + branch_signs[step]) * outer_grad - branch_signs[step] * cross_terms[
            None, None
        ]
    return (new_density, outer_grad, totals)


def local(density, hamiltonian, offsets, branch):
    moduli = jnp.array([lax.axis_size("row"), lax.axis_size("col"), density.shape[3]], jnp.int32)
    nonzero = jnp.any(offsets != 0, axis=1)
    summed = offsets[:, None, :] + offsets[None, :, :]
    differ = summed[None, :, :, :] - offsets[:, None, None, :]
    matches = jnp.all(differ % moduli == 0, axis=-1)
    closed = matches & nonzero[:, None, None] & nonzero[None, :, None] & nonzero[None, None, :]
    return lax.cond(jnp.any(closed), general_path, sparse_path, density, hamiltonian, offsets, branch)


def solution(mesh):
    return jax.shard_map(
        local,
        mesh=mesh,
        in_specs=(
            P("row", "col", None, None, None, None),
            P("row", "col", None, None, None, None),
            P(),
            P(),
        ),
        out_specs=(
            P("row", "col", None, None, None, None),
            P("row", "col", None, None, None, None),
            P(),
        ),
        check_vma=False,
    )
```

```python
import types

import jax
import jax.numpy as jnp
from jax import lax
from jax.experimental import pallas as pl
from jax.experimental.pallas import tpu as pltpu
from jax.sharding import PartitionSpec as P

F32 = jnp.float32
BF16 = jnp.bfloat16
EXTRA = 8
SIDES = ("col_far", "col_near", "row_near", "row_far")


def iotas(size):
    shape = (size, size)
    return lax.broadcasted_iota(jnp.int32, shape, 0), lax.broadcasted_iota(jnp.int32, shape, 1)


def store_split(dst, index, value):
    size = value.shape[-1]
    high = value.astype(BF16)
    dst[index + (slice(None), slice(0, size))] = high
    dst[index + (slice(None), slice(size, 2 * size))] = (value - high.astype(F32)).astype(BF16)


def split_all(src, dst):
    for t in range(src.shape[0]):
        for s in range(src.shape[1]):
            store_split(dst, (t, s), src[t, s])


def quadrants(q):
    size = q.shape[-1] // 2
    return (q[:size, :size] + q[size:, size:]) + (q[:size, size:] + q[size:, :size])


def edge_product(lefts, rights):
    size = lefts[0].shape[0]
    high = [x[:, :size] for x in lefts]
    low = [x[:, size:] for x in lefts]
    lhs = jnp.concatenate([jnp.concatenate(high, 1), jnp.concatenate(low, 1)], 0)
    rhs = jnp.concatenate(rights, 0)
    return quadrants(jnp.dot(lhs, rhs, preferred_element_type=F32))


def turned(value):
    size = value.shape[0]
    parts = [value[:, :size], value[:, size:]]
    return jnp.concatenate([x.astype(F32).T.astype(BF16) for x in parts], 1)


def symmetric(value):
    return value + value.T


def pack_pair(first, second):
    size = first.shape[-1]
    row, col = iotas(size)
    body = jnp.where(row <= col, first, second)
    diagonal = jnp.sum(jnp.where(row == col, second, 0.0), axis=0, keepdims=True)
    return jnp.concatenate([body, jnp.broadcast_to(diagonal, (EXTRA, size))], axis=0)


def unpack_pair(packed):
    size = packed.shape[-1]
    row, col = iotas(size)
    body = packed[:size]
    other = body.T
    second_diagonal = packed[size : size + 1]
    first = jnp.where(row <= col, body, other)
    second = jnp.where(row > col, body, jnp.where(row == col, second_diagonal, other))
    return first, second


def put_pairs(ref, which, blocks):
    for k in range(len(blocks) // 2):
        ref[which, k] = pack_pair(blocks[2 * k], blocks[2 * k + 1])


def put_row(refs, value):
    size = value.shape[-1]
    for ref in refs:
        ref[0, 0, size + 1 : size + 2, :] = value


def get_row(ref):
    size = ref.shape[-1]
    return ref[0, 0, size + 1 : size + 2, :]


def odd(axis):
    return lax.rem(lax.axis_index(axis), 2)


def wrap(layer, layers):
    return lax.rem(layer + 2 * layers, layers)


def slot_offsets(off, t, layers):
    return off[t, 0], off[t, 1], lax.rem(off[t, 2] + layers, layers)


def zero_slot(off, slots):
    z = jnp.int32(0)
    for t in range(slots):
        hit = (off[t, 0] == 0) & (off[t, 1] == 0) & (off[t, 2] == 0)
        z = jnp.where(hit, jnp.int32(t), z)
    return z


def sign_of(branch, k):
    return (2 * branch[k] - 1).astype(F32)


def closes(off, slots, layers, rows, cols):
    def code(r, c, l):
        return (r + 1) * (3 * layers) + (c + 1) * layers + l

    held = jnp.int32(0)
    places = []
    for t in range(slots):
        r, c, l = slot_offsets(off, t, layers)
        nonzero = (r != 0) | (c != 0) | (l != 0)
        held = held | jnp.where(nonzero, jnp.left_shift(jnp.int32(1), code(r, c, l)), 0)
        places.append((r, c, l, nonzero))
    found = jnp.int32(0)
    for i in range(slots):
        for j in range(i + 1):
            (r, c, l, some), (r2, c2, l2, some2) = places[i], places[j]
            r3 = lax.rem(r + r2 + 1 + rows, rows) - 1
            c3 = lax.rem(c + c2 + 1 + cols, cols) - 1
            l3 = lax.rem(l + l2, layers)
            inside = (r3 <= 1) & (c3 <= 1) & some & some2
            place = jnp.where(inside, code(r3, c3, l3), 0)
            hit = jnp.right_shift(held, place) & 1
            found = found | jnp.where(inside, hit, 0)
    return found


def triangle(off, slots, layers):
    def find(test):
        place = jnp.int32(0)
        for t in range(slots):
            place = jnp.where(test(off[t, 0], off[t, 1]), jnp.int32(t), place)
        return place

    g = types.SimpleNamespace()
    g.a = [find(lambda r, c, d=d: (r == d) & (c == 0)) for d in (-1, 1)]
    g.c = [find(lambda r, c, d=d: (r == d) & (c != 0)) for d in (-1, 1)]
    g.beta = off[g.c[1], 1]
    g.b = [find(lambda r, c, d=d: (r == 0) & (c == d * g.beta)) for d in (-1, 1)]
    g.la, g.lb, g.lc = (lax.rem(off[x[1], 2] + layers, layers) for x in (g.a, g.b, g.c))
    return g


def pick(pair, index):
    return jnp.where(index > 0, pair[1], pair[0])


def vertex_sums(off, left, right, acc):
    slots, layers = left.shape[0], left.shape[1]
    acc[...] = jnp.zeros_like(acc)
    for t in range(slots):
        r, _, l = slot_offsets(off, t, layers)
        for s in range(layers):
            q = lax.dot_general(
                left[t, s], right[t, s], (((0,), (0,)), ((), ())), preferred_element_type=F32
            )
            acc[r + 1, lax.rem(s + l, layers)] += quadrants(q)


def send_sums(acc, which, near, far, sym):
    layers = acc.shape[1]
    parity = odd("row")
    for r, ref in ((2 - 2 * parity, near), (2 * parity, far)):
        blocks = [acc[r, s] for s in range(layers)]
        put_pairs(ref, which, [symmetric(b) for b in blocks] if sym else blocks)


def add_sums(value, near, far, which):
    out = list(value)
    for k in range(len(out) // 2):
        for message in (near, far):
            first, second = unpack_pair(message[which, k])
            out[2 * k] = out[2 * k] + first
            out[2 * k + 1] = out[2 * k + 1] + second
    return out


def fill_neighbours(dst, own, near, far, parity, blocks):
    for k in range(dst.shape[1] // 2):
        for slot, message in ((2 - 2 * parity, near), (2 * parity, far)):
            first, second = blocks(message, k)
            store_split(dst, (slot, 2 * k), first)
            store_split(dst, (slot, 2 * k + 1), second)
    for s in range(dst.shape[1]):
        store_split(dst, (1, s), own[s])


def diagonal_blocks(k, name, own, rows, cols, which):
    def blocks(message, pair):
        return unpack_pair(message[which, pair])

    side = messages(k, name)
    fill_neighbours(rows, own, side["row_near"], side["row_far"], odd("row"), blocks)
    fill_neighbours(cols, own, side["col_near"], side["col_far"], odd("col"), blocks)


def messages(k, name):
    return {side: getattr(k, name + "_" + side) for side in SIDES}


def closed_send(k, out, f32, left, right, cross, sums_at, edges_at):
    slots, layers = left.shape[0], left.shape[1]
    g = triangle(k.off, slots, layers)
    side = messages(k, out)

    def two(x, y):
        lefts, rights = x(left), y(right)
        if not cross:
            return edge_product([lefts], [rights])
        return edge_product([lefts, x(right)], [rights, y(left)])

    parity = odd("row")
    for index, ref in ((1 - parity, side["row_near"]), (parity, side["row_far"])):
        d = 2 * index - 1
        b, c, other = pick(g.b, index), pick(g.c, index), pick(g.b, 1 - index)
        for s in range(layers):
            m = wrap(s - d * g.lc, layers)
            if sums_at is not None:
                ref[sums_at, s] = two(lambda x: turned(x[c, m]), lambda x: x[b, m])
            if edges_at is not None:
                ref[edges_at, s] = f32[other, s]
    parity = odd("col")
    for d, ref in ((1 - 2 * parity, side["col_near"]), (2 * parity - 1, side["col_far"])):
        sigma = d * g.beta
        index = (sigma + 1) // 2
        a, other, c = pick(g.a, index), pick(g.a, 1 - index), pick(g.c, 1 - index)
        for s in range(layers):
            m = wrap(s + sigma * g.lb, layers)
            if sums_at is not None:
                ref[sums_at, s] = two(lambda x: x[other, s], lambda x: turned(x[c, m]))
            if edges_at is not None:
                ref[edges_at, s] = f32[a, s]


def closed_edges(k, name, near_a, near_b, value):
    layers = near_a.shape[1]
    g = triangle(k.off, k.off.shape[0], layers)
    side = messages(k, name)
    parity = odd("row")
    for index, key in ((1 - parity, "row_near"), (parity, "row_far")):
        for s in range(layers):
            store_split(near_b, (index, s), value(side[key], key, s))
    parity = odd("col")
    for d, key in ((1 - 2 * parity, "col_near"), (2 * parity - 1, "col_far")):
        index = (1 - d * g.beta) // 2
        for s in range(layers):
            store_split(near_a, (index, s), value(side[key], key, s))


def closed_terms(k, name, terms, value, lefts, rights):
    layers = terms.shape[1]
    g = triangle(k.off, k.off.shape[0], layers)
    side = messages(k, name)
    came = {}
    parity = odd("row")
    for index, key in ((1 - parity, "row_near"), (parity, "row_far")):
        for s in range(layers):
            k.came_a[index, s] = value(side[key], key, s)
    parity = odd("col")
    for d, key in ((1 - 2 * parity, "col_near"), (2 * parity - 1, "col_far")):
        index = (1 - d * g.beta) // 2
        for s in range(layers):
            k.came_b[index, s] = value(side[key], key, s)
    for index in (0, 1):
        sigma = 2 * index - 1
        a, b, c = g.a[index], g.b[index], g.c[index]

        def product(x, y):
            return edge_product([x(*left) for left in lefts], [y(*right) for right in rights])

        for s in range(layers):
            back, on, up = (wrap(s + m, layers) for m in (-sigma * g.lb, sigma * g.lb, sigma * g.la))
            terms[a, s] = k.came_a[index, s] + product(
                lambda f, ea, eb: turned(f[b, back]), lambda f, ea, eb: f[c, back]
            )
            terms[b, s] = k.came_b[index, s] + product(
                lambda f, ea, eb: f[c, s], lambda f, ea, eb: turned(f[a, on])
            )
            terms[c, s] = product(lambda f, ea, eb: f[b, s], lambda f, ea, eb: f[a, on]) + product(
                lambda f, ea, eb: ea[index, s], lambda f, ea, eb: eb[index, up]
            )


def start_kernel(rows, cols, k):
    slots, layers = k.x.shape[0], k.x.shape[1]
    z = zero_slot(k.off, slots)
    for t in range(slots):
        for j in range(3):
            k.table[t, j] = k.off[t, j]
    k.flag[0] = closes(k.off, slots, layers, rows, cols)
    split_all(k.x, k.xs)
    vertex_sums(k.off, k.xs, k.xs, k.acc)
    for ref in (k.near, k.far, k.side):
        put_pairs(ref, 0, [k.x[z, s] for s in range(layers)])
        put_pairs(ref, 1, [k.h[z, s] for s in range(layers)])
    send_sums(k.acc, 2, k.near, k.far, False)
    for s in range(layers):
        k.local[s] = k.acc[1, s]


def closed_start_kernel(k):
    split_all(k.x, k.xs)
    closed_send(k, "out", k.x, k.xs, k.xs, False, 0, 1)
    closed_send(k, "out", k.h, k.xs, k.xs, False, None, 2)


def square_step(k, step, sums_at, closed):
    slots, layers = k.x.shape[0], k.x.shape[1]
    s_k = sign_of(k.branch, step)
    z = zero_slot(k.off, slots)
    split_all(k.x, k.xs)
    own = [k.x[z, s] for s in range(layers)]
    diagonal_blocks(k, "m", own, k.x_rows, k.x_cols, 0)
    square = add_sums([k.x_local[s] for s in range(layers)], k.m_row_near, k.m_row_far, sums_at)
    for s in range(layers):
        k.new[z, s] = own[s] + s_k * (own[s] - square[s])
    if closed:
        closed_edges(k, "e", k.x_near_a, k.x_near_b, lambda ref, key, s: ref[1, s])
        operand = [(k.xs, k.x_near_a, k.x_near_b)]
        closed_terms(k, "e", k.terms, lambda ref, key, s: ref[0, s], operand, operand)
    for i in range(slots - 1):
        t = i + (i >= z).astype(jnp.int32)
        r, c, l = slot_offsets(k.off, t, layers)
        for s in range(layers):
            e = k.xs[t, s]
            product = edge_product([k.x_cols[1 - c, s], e], [e, k.x_rows[1 + r, lax.rem(s + l, layers)]])
            if closed:
                product = product + k.terms[t, s]
            e32 = k.x[t, s]
            k.new[t, s] = e32 + s_k * (e32 - product)
    return z


def square_kernel(step, sums_at, closed, k):
    layers = k.x.shape[1]
    z = square_step(k, step, sums_at, closed)
    for ref in (k.near, k.far, k.side):
        put_pairs(ref, 0, [k.new[z, s] for s in range(layers)])
    split_all(k.new, k.ns)
    vertex_sums(k.off, k.ns, k.ns, k.acc)
    send_sums(k.acc, 1, k.near, k.far, False)
    for s in range(layers):
        k.local[s] = k.acc[1, s]
    if closed:
        closed_send(k, "out", k.new, k.ns, k.ns, False, 0, 1)


def turn_square_kernel(step, sums_at, closed, k):
    square_kernel(step, sums_at, closed, k)
    slots, layers, size = k.x.shape[0], k.x.shape[1], k.x.shape[2]
    z = zero_slot(k.off, slots)
    split_all(k.h, k.hs)
    vertex_sums(k.off, k.hs, k.ns, k.acc_h)
    send_sums(k.acc_h, 2, k.near, k.far, True)
    vertex_sums(k.off, k.ns, k.xs, k.acc_cross)
    send_sums(k.acc_cross, 3, k.near, k.far, True)
    for s in range(layers):
        k.h_local[s] = symmetric(k.acc_h[1, s])
        k.cross_local[s] = symmetric(k.acc_cross[1, s])
    if closed:
        closed_send(k, "out", None, k.hs, k.ns, True, 2, None)
        closed_send(k, "out", None, k.ns, k.xs, True, 3, None)
    s_next = sign_of(k.branch, step + 1)
    row, col = iotas(size)
    squares = jnp.zeros((size, size), F32)
    for t in range(slots):
        for s in range(layers):
            squares = squares + k.new[t, s] * k.new[t, s]
    trace = jnp.zeros_like(squares)
    for s in range(layers):
        trace = trace + jnp.where(row == col, k.new[z, s], 0.0)
    part = (1.0 + s_next) * trace - s_next * squares
    k.sums[...] = jnp.broadcast_to(jnp.sum(part, keepdims=True), k.sums.shape)
    put_row((k.near, k.far, k.side), k.sums[0:1, :])


def last_square_kernel(step, sums_at, closed, k):
    square_step(k, step, sums_at, closed)
    k.done[...] = jnp.zeros_like(k.done)


def gradient_edges(k, s_k, g, z, closed):
    slots, layers = g.shape[0], g.shape[1]
    for i in range(slots - 1):
        t = i + (i >= z).astype(jnp.int32)
        r, c, l = slot_offsets(k.off, t, layers)
        for s in range(layers):
            e, f = k.gs[t, s], k.xs[t, s]
            b = lax.rem(s + l, layers)
            product = edge_product(
                [k.g_cols[1 - c, s], k.x_cols[1 - c, s], e, f],
                [f, e, k.x_rows[1 + r, b], k.g_rows[1 + r, b]],
            )
            if closed:
                product = product + k.terms[t, s]
            k.new[t, s] = (1.0 + s_k) * g[t, s] - s_k * product


def gradient_terms(k, name, value):
    lefts = [(k.gs, k.g_near_a, k.g_near_b), (k.xs, k.x_near_a, k.x_near_b)]
    closed_terms(k, name, k.terms, value, lefts, lefts[::-1])


def gradient_tail(k, z, closed):
    layers = k.x.shape[1]
    for ref in (k.near, k.far, k.side):
        put_pairs(ref, 0, [k.new[z, s] for s in range(layers)])
    split_all(k.new, k.ns)
    split_all(k.before, k.bs)
    vertex_sums(k.off, k.ns, k.bs, k.acc)
    send_sums(k.acc, 1, k.near, k.far, True)
    for s in range(layers):
        k.local[s] = symmetric(k.acc[1, s])
    if closed:
        closed_send(k, "out", k.new, k.ns, k.bs, True, 0, 1)


def first_gradient_kernel(step, four, closed, k):
    layers = k.x.shape[1]
    s_k = sign_of(k.branch, step)
    z = zero_slot(k.off, k.x.shape[0])
    split_all(k.h, k.gs)
    split_all(k.x, k.xs)
    own_h = [k.h[z, s] for s in range(layers)]
    diagonal_blocks(k, "h", own_h, k.g_rows, k.g_cols, 1)
    diagonal_blocks(k, "m", [k.x[z, s] for s in range(layers)], k.x_rows, k.x_cols, 0)
    cross = add_sums([k.h_local[s] for s in range(layers)], k.m_row_near, k.m_row_far, 2)
    for s in range(layers):
        k.new[z, s] = (1.0 + s_k) * own_h[s] - s_k * cross[s]
    if closed:
        closed_edges(k, "he", k.g_near_a, k.g_near_b, lambda ref, key, s: ref[2, s])
        closed_edges(k, "e", k.x_near_a, k.x_near_b, lambda ref, key, s: ref[1, s])
        gradient_terms(k, "e", lambda ref, key, s: ref[2, s])
    gradient_edges(k, s_k, k.h, z, closed)
    gradient_tail(k, z, closed)
    energy = jnp.zeros_like(k.x[0, 0])
    for t in range(k.x.shape[0]):
        for s in range(layers):
            energy = energy + ((1.0 + s_k) * k.h[t, s] + k.new[t, s]) * k.x[t, s]
    k.sums[0:1, :] = row_sum(
        four, k.occupied[0:1, :], get_row(k.m_row_near), get_row(k.m_row_far), k.rest[0:1, :]
    )
    k.sums[1:2, :] = jnp.broadcast_to(0.5 * jnp.sum(energy, keepdims=True), (1, k.sums.shape[1]))
    k.sums[2:, :] = jnp.zeros_like(k.sums[2:, :])


def next_gradient_kernel(step, order, closed, k):
    slots, layers, size = k.x.shape[0], k.x.shape[1], k.x.shape[2]
    s_k = sign_of(k.branch, step)
    s_after = sign_of(k.branch, step + 1)
    sums = k.sums[...] + k.done[...]
    k.passed[...] = sums
    excess = sums[0:1, :] * (1.0 / order) - 0.5
    z = zero_slot(k.off, slots)
    row, col = iotas(size)
    eye = jnp.where(row == col, excess * (1.0 + s_after), 0.0)
    scale = excess * (-2.0 * s_after)
    for t in range(slots):
        for s in range(layers):
            k.g[t, s] = k.gh[t, s] + scale * k.after[t, s]
    for s in range(layers):
        k.g[z, s] = k.g[z, s] + eye
    split_all(k.g, k.gs)
    split_all(k.x, k.xs)
    own_g = [k.g[z, s] for s in range(layers)]
    own_x = [k.x[z, s] for s in range(layers)]

    def blocks(message, pair):
        now, then = (unpack_pair(m[0, pair]) for m in message)
        return [a + scale * b + eye for a, b in zip(now, then)]

    gm, am = messages(k, "gm"), messages(k, "am")
    both = {side: (gm[side], am[side]) for side in SIDES}
    fill_neighbours(k.g_rows, own_g, both["row_near"], both["row_far"], odd("row"), blocks)
    fill_neighbours(k.g_cols, own_g, both["col_near"], both["col_far"], odd("col"), blocks)
    diagonal_blocks(k, "m", own_x, k.x_rows, k.x_cols, 0)
    own_sums = add_sums([k.g_local[s] for s in range(layers)], k.gm_row_near, k.gm_row_far, 1)
    cross_sums = add_sums([k.cross_local[s] for s in range(layers)], k.am_row_near, k.am_row_far, 3)
    twice = 2.0 * (1.0 + s_after) * excess
    for s in range(layers):
        cross = own_sums[s] + scale * cross_sums[s] + twice * own_x[s]
        k.new[z, s] = (1.0 + s_k) * own_g[s] - s_k * cross
    if closed:
        ae = messages(k, "ae")
        closed_edges(
            k, "ge", k.g_near_a, k.g_near_b, lambda ref, key, s: ref[1, s] + scale * ae[key][1, s]
        )
        closed_edges(k, "e", k.x_near_a, k.x_near_b, lambda ref, key, s: ref[1, s])
        gradient_terms(k, "ge", lambda ref, key, s: ref[0, s] + scale * ae[key][3, s])
    gradient_edges(k, s_k, k.g, z, closed)
    gradient_tail(k, z, closed)
    k.energy[...] = jnp.broadcast_to(sums[1:2, :], k.energy.shape)
    put_row((k.near, k.far, k.side), sums[1:2, :])


def last_gradient_kernel(step, order, four, closed, k):
    layers = k.x.shape[1]
    s_k = sign_of(k.branch, step)
    z = zero_slot(k.off, k.x.shape[0])
    split_all(k.g, k.gs)
    split_all(k.x, k.xs)
    own_g = [k.g[z, s] for s in range(layers)]
    diagonal_blocks(k, "gm", own_g, k.g_rows, k.g_cols, 0)
    diagonal_blocks(k, "m", [k.x[z, s] for s in range(layers)], k.x_rows, k.x_cols, 0)
    cross = add_sums([k.g_local[s] for s in range(layers)], k.gm_row_near, k.gm_row_far, 1)
    for s in range(layers):
        k.new[z, s] = (1.0 + s_k) * own_g[s] - s_k * cross[s]
    if closed:
        closed_edges(k, "ge", k.g_near_a, k.g_near_b, lambda ref, key, s: ref[1, s])
        closed_edges(k, "e", k.x_near_a, k.x_near_b, lambda ref, key, s: ref[1, s])
        gradient_terms(k, "ge", lambda ref, key, s: ref[0, s])
    gradient_edges(k, s_k, k.g, z, closed)
    energy = row_sum(four, k.energy[...], get_row(k.gm_row_near), get_row(k.gm_row_far), k.rest[...])
    lane = lax.broadcasted_iota(jnp.int32, k.totals.shape, 1)
    k.totals[...] = jnp.where(lane == 0, energy, k.sums[0:1, :]) * (1.0 / order)


def call(kernel, smem, vmem, outs, scratch, smem_outs=()):
    names = [*smem, *vmem, *outs, *dict(smem_outs), *scratch]
    small = dict(smem_outs)

    def body(*refs):
        kernel(types.SimpleNamespace(**dict(zip(names, refs))))

    results = pl.pallas_call(
        body,
        out_shape=[jax.ShapeDtypeStruct(shape, F32) for shape in outs.values()]
        + [jax.ShapeDtypeStruct(shape, jnp.int32) for shape in small.values()],
        in_specs=[pl.BlockSpec(memory_space=pltpu.SMEM)] * len(smem)
        + [pl.BlockSpec(memory_space=pltpu.VMEM)] * len(vmem),
        out_specs=[pl.BlockSpec(memory_space=pltpu.VMEM)] * len(outs)
        + [pl.BlockSpec(memory_space=pltpu.SMEM)] * len(small),
        scratch_shapes=list(scratch.values()),
        compiler_params=pltpu.CompilerParams(vmem_limit_bytes=40 * 1024 * 1024),
    )(*smem.values(), *vmem.values())
    return types.SimpleNamespace(**dict(zip([*outs, *small], results)))


def pairs_of(axis):
    count = lax.axis_size(axis)
    near = [(i, i ^ 1) for i in range(count)]
    far = [(i, (i - 1) % count if i % 2 == 0 else (i + 1) % count) for i in range(count)]
    return near, far


def swap(col_far, col_near, row_near, row_far):
    near_row, far_row = pairs_of("row")
    near_col, far_col = pairs_of("col")
    return dict(
        col_far=lax.ppermute(col_far, "col", far_col),
        col_near=lax.ppermute(col_near, "col", near_col),
        row_near=lax.ppermute(row_near, "row", near_row),
        row_far=lax.ppermute(row_far, "row", far_row),
    )


def exchange(k):
    return swap(k.side, k.side, k.near, k.far)


def exchange_edges(k):
    return swap(k.out_col_far, k.out_col_near, k.out_row_near, k.out_row_far)


def named(name, arrays):
    return {name + "_" + side: arrays[side] for side in SIDES}


def total_over(value, axis):
    count = lax.axis_size(axis)
    if count & (count - 1):
        return lax.psum(value, axis)
    step = 1
    while step < count:
        value = value + lax.ppermute(value, axis, [(i, i ^ step) for i in range(count)])
        step *= 2
    return value


def four_rows():
    return lax.axis_size("row") == 4


def row_remainder(value):
    if four_rows():
        return lax.ppermute(value, "row", [(i, i ^ 2) for i in range(4)])
    return total_over(value, "row")


def row_sum(four, own, near, far, rest):
    return (own + near) + (far + rest) if four else rest


class Shapes:
    def __init__(self, density):
        slots, layers, size = density.shape[2:5]
        self.full = (slots, layers, size, size)
        self.local = (layers, size, size)
        self.tile = (8, size)
        self.order = float(size * layers * lax.axis_size("row") * lax.axis_size("col"))
        self.split = pltpu.VMEM((slots, layers, size, 2 * size), BF16)
        self.three = pltpu.VMEM((3, layers, size, 2 * size), BF16)
        self.two = pltpu.VMEM((2, layers, size, 2 * size), BF16)
        self.two_wide = pltpu.VMEM((2, layers, size, size), F32)
        self.acc = pltpu.VMEM((3, layers, size, size), F32)
        self.wide = pltpu.VMEM(self.full, F32)
        self.pairs = (layers // 2, size + EXTRA, size)

    def messages(self, rows, cols):
        return dict(near=(rows, *self.pairs), far=(rows, *self.pairs), side=(cols, *self.pairs))

    def edges(self, count, closed):
        return {"out_" + side: (count, *self.local) for side in SIDES} if closed else {}

    def near_edges(self, names, closed):
        if not closed:
            return {}
        out = dict(terms=self.wide, came_a=self.two_wide, came_b=self.two_wide)
        for name in names:
            out[name + "_near_a"] = self.two
            out[name + "_near_b"] = self.two
        return out


def steps(closed, x0, h, table, branch, local0, near0):
    shape = Shapes(x0[None, None])
    full, local, tile, order = shape.full, shape.local, shape.tile, shape.order
    split, three, acc = shape.split, shape.three, shape.acc
    smem = dict(off=table, branch=branch)
    four = four_rows()
    square_scratch = dict(xs=split, x_rows=three, x_cols=three, **shape.near_edges(["x"], closed))
    pair_scratch = dict(
        gs=split, xs=split, g_rows=three, g_cols=three, x_rows=three, x_cols=three,
        **shape.near_edges(["g", "x"], closed),
    )
    tail = dict(ns=split, bs=split, acc=acc)

    def edges(**fields):
        out = {}
        for name, arrays in fields.items():
            out.update(named(name, arrays) if closed else {})
        return out

    edge0 = edge1 = edge2 = edge_gh = edge_g1 = None
    if closed:
        k = call(closed_start_kernel, dict(off=table), dict(x=x0, h=h), shape.edges(3, True), dict(xs=split))
        edge0 = exchange_edges(k)
    k = call(
        lambda k: square_kernel(0, 2, closed, k), smem,
        dict(x=x0, x_local=local0, **named("m", near0), **edges(e=edge0)),
        dict(new=full, local=local, **shape.messages(2, 1), **shape.edges(2, closed)),
        dict(ns=split, acc=acc, **square_scratch),
    )
    x1, local1, near1 = k.new, k.local, exchange(k)
    if closed:
        edge1 = exchange_edges(k)
    k = call(
        lambda k: turn_square_kernel(1, 1, closed, k), smem,
        dict(x=x1, x_local=local1, h=h, **named("m", near1), **edges(e=edge1)),
        dict(new=full, local=local, h_local=local, cross_local=local, sums=tile,
             **shape.messages(4, 1), **shape.edges(4, closed)),
        dict(ns=split, hs=split, acc=acc, acc_h=acc, acc_cross=acc, **square_scratch),
    )
    x2, local2, h_local, cross_local, occupied, near2 = (
        k.new, k.local, k.h_local, k.cross_local, k.sums, exchange(k)
    )
    if closed:
        edge2 = exchange_edges(k)
    rest = row_remainder(occupied)
    k = call(
        lambda k: first_gradient_kernel(2, four, closed, k), smem,
        dict(h=h, x=x2, before=x1, h_local=h_local, **named("h", near0), **named("m", near2),
             occupied=occupied, rest=rest, **edges(he=edge0, e=edge2)),
        dict(new=full, local=local, sums=tile, **shape.messages(2, 1), **shape.edges(2, closed)),
        dict(**pair_scratch, **tail),
    )
    gh, gh_local, sums, near_gh = k.new, k.local, k.sums, exchange(k)
    if closed:
        edge_gh = exchange_edges(k)
    sums = total_over(sums, "col")
    k = call(
        lambda k: last_square_kernel(2, 1, closed, k), smem,
        dict(**named("m", near2), x=x2, x_local=local2, **edges(e=edge2)),
        dict(new=full, done=tile), square_scratch,
    )
    x3, done = k.new, k.done
    k = call(
        lambda k: next_gradient_kernel(1, order, closed, k), smem,
        dict(sums=sums, done=done, gh=gh, after=x2, x=x1, before=x0, g_local=gh_local,
             cross_local=cross_local, **named("gm", near_gh), **named("am", near2), **named("m", near1),
             **edges(ge=edge_gh, ae=edge2, e=edge1)),
        dict(new=full, local=local, passed=tile, energy=tile,
             **shape.messages(2, 1), **shape.edges(2, closed)),
        dict(g=shape.wide, **pair_scratch, **tail),
    )
    g1, g1_local, sums, energy, near_g1 = k.new, k.local, k.passed, k.energy, exchange(k)
    if closed:
        edge_g1 = exchange_edges(k)
    rest = row_remainder(energy)
    k = call(
        lambda k: last_gradient_kernel(0, order, four, closed, k), smem,
        dict(sums=sums, energy=energy, rest=rest, g=g1, x=x0, g_local=g1_local,
             **named("gm", near_g1), **named("m", near0), **edges(ge=edge_g1, e=edge0)),
        dict(new=full, totals=tile), pair_scratch,
    )
    return x3, k.new, k.totals


def local(density, hamiltonian, offsets, branch):
    shape = Shapes(density)
    x0 = density.reshape(shape.full)
    h = hamiltonian.reshape(shape.full)
    rows, cols = lax.axis_size("row"), lax.axis_size("col")
    k = call(
        lambda k: start_kernel(rows, cols, k), dict(off=offsets), dict(x=x0, h=h),
        dict(local=shape.local, **shape.messages(3, 2)), dict(xs=shape.split, acc=shape.acc),
        dict(flag=(1,), table=offsets.shape),
    )
    near0 = exchange(k)
    x3, g0, totals = lax.cond(
        k.flag[0] > 0, lambda *a: steps(True, *a), lambda *a: steps(False, *a),
        x0, h, k.table, branch, k.local, near0,
    )
    return x3.reshape(density.shape), g0.reshape(density.shape), totals[0, :2]


def solution(mesh):
    return jax.shard_map(
        local,
        mesh=mesh,
        in_specs=(
            P("row", "col", None, None, None, None),
            P("row", "col", None, None, None, None),
            P(),
            P(),
        ),
        out_specs=(
            P("row", "col", None, None, None, None),
            P("row", "col", None, None, None, None),
            P(),
        ),
        check_vma=False,
    )
```

```python
import types

import jax
import jax.numpy as jnp
from jax import lax
from jax.experimental import pallas as pl
from jax.experimental.pallas import tpu as pltpu
from jax.sharding import PartitionSpec as P

F32 = jnp.float32
BF16 = jnp.bfloat16
EXTRA = 8
SIDES = ("col_far", "col_near", "row_near", "row_far")


def each(count, body, rolled):
    if not rolled:
        for i in range(count):
            body(i)
        return

    def step(i, carry):
        body(i)
        return carry

    lax.fori_loop(0, count, step, 0)


def total_of(count, term, first, rolled):
    if not rolled:
        for i in range(count):
            first = first + term(i)
        return first
    return lax.fori_loop(0, count, lambda i, sum_: sum_ + term(i), first)


def iotas(size):
    shape = (size, size)
    return lax.broadcasted_iota(jnp.int32, shape, 0), lax.broadcasted_iota(jnp.int32, shape, 1)


def store_split(dst, index, value):
    size = value.shape[-1]
    high = value.astype(BF16)
    dst[index + (slice(None), slice(0, size))] = high
    dst[index + (slice(None), slice(size, 2 * size))] = (value - high.astype(F32)).astype(BF16)


def split_all(src, dst, rolled):
    layers = src.shape[1]

    def one(i):
        t, s = i // layers, i % layers
        store_split(dst, (t, s), src[t, s])

    each(src.shape[0] * layers, one, rolled)


def quadrants(q):
    size = q.shape[-1] // 2
    return (q[:size, :size] + q[size:, size:]) + (q[:size, size:] + q[size:, :size])


def edge_product(lefts, rights):
    size = lefts[0].shape[0]
    high = [x[:, :size] for x in lefts]
    low = [x[:, size:] for x in lefts]
    lhs = jnp.concatenate([jnp.concatenate(high, 1), jnp.concatenate(low, 1)], 0)
    rhs = jnp.concatenate(rights, 0)
    return quadrants(jnp.dot(lhs, rhs, preferred_element_type=F32))


def turned(value):
    size = value.shape[0]
    parts = [value[:, :size], value[:, size:]]
    return jnp.concatenate([x.astype(F32).T.astype(BF16) for x in parts], 1)


def symmetric(value):
    return value + value.T


def pack_pair(first, second):
    size = first.shape[-1]
    row, col = iotas(size)
    body = jnp.where(row <= col, first, second)
    diagonal = jnp.sum(jnp.where(row == col, second, 0.0), axis=0, keepdims=True)
    return jnp.concatenate([body, jnp.broadcast_to(diagonal, (EXTRA, size))], axis=0)


def unpack_pair(packed):
    size = packed.shape[-1]
    row, col = iotas(size)
    body = packed[:size]
    other = body.T
    second_diagonal = packed[size : size + 1]
    first = jnp.where(row <= col, body, other)
    second = jnp.where(row > col, body, jnp.where(row == col, second_diagonal, other))
    return first, second


def put_pairs(ref, which, blocks):
    for k in range(len(blocks) // 2):
        ref[which, k] = pack_pair(blocks[2 * k], blocks[2 * k + 1])


def put_row(refs, value):
    size = value.shape[-1]
    for ref in refs:
        ref[0, 0, size + 1 : size + 2, :] = value


def get_row(ref):
    size = ref.shape[-1]
    return ref[0, 0, size + 1 : size + 2, :]


def odd(axis):
    return lax.rem(lax.axis_index(axis), 2)


def wrap(layer, layers):
    return lax.rem(layer + 2 * layers, layers)


def slot_offsets(off, t, layers):
    return off[t, 0], off[t, 1], lax.rem(off[t, 2] + layers, layers)


def zero_slot(off, slots):
    z = jnp.int32(0)
    for t in range(slots):
        hit = (off[t, 0] == 0) & (off[t, 1] == 0) & (off[t, 2] == 0)
        z = jnp.where(hit, jnp.int32(t), z)
    return z


def sign_of(branch, k):
    return (2 * branch[k] - 1).astype(F32)


def closes(off, slots, layers, rows, cols):
    def code(r, c, l):
        return (r + 1) * (3 * layers) + (c + 1) * layers + l

    held = jnp.int32(0)
    places = []
    for t in range(slots):
        r, c, l = slot_offsets(off, t, layers)
        nonzero = (r != 0) | (c != 0) | (l != 0)
        held = held | jnp.where(nonzero, jnp.left_shift(jnp.int32(1), code(r, c, l)), 0)
        places.append((r, c, l, nonzero))
    found = jnp.int32(0)
    for i in range(slots):
        for j in range(i + 1):
            (r, c, l, some), (r2, c2, l2, some2) = places[i], places[j]
            r3 = lax.rem(r + r2 + 1 + rows, rows) - 1
            c3 = lax.rem(c + c2 + 1 + cols, cols) - 1
            l3 = lax.rem(l + l2, layers)
            inside = (r3 <= 1) & (c3 <= 1) & some & some2
            place = jnp.where(inside, code(r3, c3, l3), 0)
            hit = jnp.right_shift(held, place) & 1
            found = found | jnp.where(inside, hit, 0)
    return found


def triangle(off, slots, layers):
    def find(test):
        place = jnp.int32(0)
        for t in range(slots):
            place = jnp.where(test(off[t, 0], off[t, 1]), jnp.int32(t), place)
        return place

    g = types.SimpleNamespace()
    g.a = [find(lambda r, c, d=d: (r == d) & (c == 0)) for d in (-1, 1)]
    g.c = [find(lambda r, c, d=d: (r == d) & (c != 0)) for d in (-1, 1)]
    g.beta = off[g.c[1], 1]
    g.b = [find(lambda r, c, d=d: (r == 0) & (c == d * g.beta)) for d in (-1, 1)]
    g.la, g.lb, g.lc = (lax.rem(off[x[1], 2] + layers, layers) for x in (g.a, g.b, g.c))
    return g


def pick(pair, index):
    return jnp.where(index > 0, pair[1], pair[0])


def vertex_sums(off, left, right, acc, rolled):
    slots, layers = left.shape[0], left.shape[1]
    acc[...] = jnp.zeros_like(acc)

    def add(i):
        t, s = i // layers, i % layers
        r, _, l = slot_offsets(off, t, layers)
        q = lax.dot_general(
            left[t, s], right[t, s], (((0,), (0,)), ((), ())), preferred_element_type=F32
        )
        acc[r + 1, lax.rem(s + l, layers)] += quadrants(q)

    each(slots * layers, add, rolled)


def send_sums(acc, which, near, far, sym):
    layers = acc.shape[1]
    parity = odd("row")
    for r, ref in ((2 - 2 * parity, near), (2 * parity, far)):
        blocks = [acc[r, s] for s in range(layers)]
        put_pairs(ref, which, [symmetric(b) for b in blocks] if sym else blocks)


def add_sums(value, near, far, which):
    out = list(value)
    for k in range(len(out) // 2):
        for message in (near, far):
            first, second = unpack_pair(message[which, k])
            out[2 * k] = out[2 * k] + first
            out[2 * k + 1] = out[2 * k + 1] + second
    return out


def fill_neighbours(dst, own, near, far, parity, blocks):
    for k in range(dst.shape[1] // 2):
        for slot, message in ((2 - 2 * parity, near), (2 * parity, far)):
            first, second = blocks(message, k)
            store_split(dst, (slot, 2 * k), first)
            store_split(dst, (slot, 2 * k + 1), second)
    for s in range(dst.shape[1]):
        store_split(dst, (1, s), own[s])


def diagonal_blocks(k, name, own, rows, cols, which):
    def blocks(message, pair):
        return unpack_pair(message[which, pair])

    side = messages(k, name)
    fill_neighbours(rows, own, side["row_near"], side["row_far"], odd("row"), blocks)
    fill_neighbours(cols, own, side["col_near"], side["col_far"], odd("col"), blocks)


def messages(k, name):
    return {side: getattr(k, name + "_" + side) for side in SIDES}


def closed_send(k, out, f32, left, right, cross, sums_at, edges_at):
    slots, layers = left.shape[0], left.shape[1]
    g = triangle(k.off, slots, layers)
    side = messages(k, out)

    def two(x, y):
        lefts, rights = x(left), y(right)
        if not cross:
            return edge_product([lefts], [rights])
        return edge_product([lefts, x(right)], [rights, y(left)])

    parity = odd("row")
    for index, ref in ((1 - parity, side["row_near"]), (parity, side["row_far"])):
        d = 2 * index - 1
        b, c, other = pick(g.b, index), pick(g.c, index), pick(g.b, 1 - index)

        def row_blocks(s, ref=ref, d=d, b=b, c=c, other=other):
            m = wrap(s - d * g.lc, layers)
            if sums_at is not None:
                ref[sums_at, s] = two(lambda x: turned(x[c, m]), lambda x: x[b, m])
            if edges_at is not None:
                ref[edges_at, s] = f32[other, s]

        each(layers, row_blocks, True)
    parity = odd("col")
    for d, ref in ((1 - 2 * parity, side["col_near"]), (2 * parity - 1, side["col_far"])):
        sigma = d * g.beta
        index = (sigma + 1) // 2
        a, other, c = pick(g.a, index), pick(g.a, 1 - index), pick(g.c, 1 - index)

        def col_blocks(s, ref=ref, sigma=sigma, a=a, other=other, c=c):
            m = wrap(s + sigma * g.lb, layers)
            if sums_at is not None:
                ref[sums_at, s] = two(lambda x: x[other, s], lambda x: turned(x[c, m]))
            if edges_at is not None:
                ref[edges_at, s] = f32[a, s]

        each(layers, col_blocks, True)


def closed_edges(k, name, near_a, near_b, value):
    layers = near_a.shape[1]
    g = triangle(k.off, k.off.shape[0], layers)
    side = messages(k, name)
    parity = odd("row")
    for index, key in ((1 - parity, "row_near"), (parity, "row_far")):
        each(
            layers,
            lambda s, i=index, key=key: store_split(near_b, (i, s), value(side[key], key, s)),
            True,
        )
    parity = odd("col")
    for d, key in ((1 - 2 * parity, "col_near"), (2 * parity - 1, "col_far")):
        index = (1 - d * g.beta) // 2
        each(
            layers,
            lambda s, i=index, key=key: store_split(near_a, (i, s), value(side[key], key, s)),
            True,
        )


def closed_terms(k, name, terms, value, lefts, rights):
    layers = terms.shape[1]
    g = triangle(k.off, k.off.shape[0], layers)
    side = messages(k, name)
    parity = odd("row")
    for index, key in ((1 - parity, "row_near"), (parity, "row_far")):
        for s in range(layers):
            k.came_a[index, s] = value(side[key], key, s)
    parity = odd("col")
    for d, key in ((1 - 2 * parity, "col_near"), (2 * parity - 1, "col_far")):
        index = (1 - d * g.beta) // 2
        for s in range(layers):
            k.came_b[index, s] = value(side[key], key, s)

    def product(x, y):
        return edge_product([x(*left) for left in lefts], [y(*right) for right in rights])

    def corner(i):
        index, s = i // layers, i % layers
        sigma = 2 * index - 1
        a, b, c = pick(g.a, index), pick(g.b, index), pick(g.c, index)
        back, on, up = (wrap(s + m, layers) for m in (-sigma * g.lb, sigma * g.lb, sigma * g.la))
        terms[a, s] = k.came_a[index, s] + product(
            lambda f, ea, eb: turned(f[b, back]), lambda f, ea, eb: f[c, back]
        )
        terms[b, s] = k.came_b[index, s] + product(
            lambda f, ea, eb: f[c, s], lambda f, ea, eb: turned(f[a, on])
        )
        terms[c, s] = product(lambda f, ea, eb: f[b, s], lambda f, ea, eb: f[a, on]) + product(
            lambda f, ea, eb: ea[index, s], lambda f, ea, eb: eb[index, up]
        )

    each(2 * layers, corner, True)


def start_kernel(rows, cols, k):
    slots, layers = k.x.shape[0], k.x.shape[1]
    z = zero_slot(k.off, slots)
    for t in range(slots):
        for j in range(3):
            k.table[t, j] = k.off[t, j]
    k.flag[0] = closes(k.off, slots, layers, rows, cols)
    split_all(k.x, k.xs, False)
    vertex_sums(k.off, k.xs, k.xs, k.acc, False)
    for ref in (k.near, k.far, k.side):
        put_pairs(ref, 0, [k.x[z, s] for s in range(layers)])
        put_pairs(ref, 1, [k.h[z, s] for s in range(layers)])
    send_sums(k.acc, 2, k.near, k.far, False)
    for s in range(layers):
        k.local[s] = k.acc[1, s]


def closed_start_kernel(k):
    split_all(k.x, k.xs, True)
    closed_send(k, "out", k.x, k.xs, k.xs, False, 0, 1)
    closed_send(k, "out", k.h, k.xs, k.xs, False, None, 2)


def square_step(k, step, sums_at, closed):
    slots, layers = k.x.shape[0], k.x.shape[1]
    s_k = sign_of(k.branch, step)
    z = zero_slot(k.off, slots)
    split_all(k.x, k.xs, closed)
    own = [k.x[z, s] for s in range(layers)]
    diagonal_blocks(k, "m", own, k.x_rows, k.x_cols, 0)
    square = add_sums([k.x_local[s] for s in range(layers)], k.m_row_near, k.m_row_far, sums_at)
    for s in range(layers):
        k.new[z, s] = own[s] + s_k * (own[s] - square[s])
    if closed:
        closed_edges(k, "e", k.x_near_a, k.x_near_b, lambda ref, key, s: ref[1, s])
        operand = [(k.xs, k.x_near_a, k.x_near_b)]
        closed_terms(k, "e", k.terms, lambda ref, key, s: ref[0, s], operand, operand)

    def edge(i):
        i, s = i // layers, i % layers
        t = i + (i >= z).astype(jnp.int32)
        r, c, l = slot_offsets(k.off, t, layers)
        e = k.xs[t, s]
        product = edge_product([k.x_cols[1 - c, s], e], [e, k.x_rows[1 + r, lax.rem(s + l, layers)]])
        if closed:
            product = product + k.terms[t, s]
        e32 = k.x[t, s]
        k.new[t, s] = e32 + s_k * (e32 - product)

    each((slots - 1) * layers, edge, closed)
    return z


def square_kernel(step, sums_at, closed, k):
    layers = k.x.shape[1]
    z = square_step(k, step, sums_at, closed)
    for ref in (k.near, k.far, k.side):
        put_pairs(ref, 0, [k.new[z, s] for s in range(layers)])
    split_all(k.new, k.ns, closed)
    vertex_sums(k.off, k.ns, k.ns, k.acc, closed)
    send_sums(k.acc, 1, k.near, k.far, False)
    for s in range(layers):
        k.local[s] = k.acc[1, s]
    if closed:
        closed_send(k, "out", k.new, k.ns, k.ns, False, 0, 1)


def turn_square_kernel(step, sums_at, closed, k):
    square_kernel(step, sums_at, closed, k)
    slots, layers, size = k.x.shape[0], k.x.shape[1], k.x.shape[2]
    z = zero_slot(k.off, slots)
    split_all(k.h, k.hs, closed)
    vertex_sums(k.off, k.hs, k.ns, k.acc_h, closed)
    send_sums(k.acc_h, 2, k.near, k.far, True)
    vertex_sums(k.off, k.ns, k.xs, k.acc_cross, closed)
    send_sums(k.acc_cross, 3, k.near, k.far, True)
    for s in range(layers):
        k.h_local[s] = symmetric(k.acc_h[1, s])
        k.cross_local[s] = symmetric(k.acc_cross[1, s])
    if closed:
        closed_send(k, "out", None, k.hs, k.ns, True, 2, None)
        closed_send(k, "out", None, k.ns, k.xs, True, 3, None)
    s_next = sign_of(k.branch, step + 1)
    row, col = iotas(size)
    squares = total_of(
        slots * layers,
        lambda i: k.new[i // layers, i % layers] * k.new[i // layers, i % layers],
        jnp.zeros((size, size), F32),
        closed,
    )
    trace = jnp.zeros_like(squares)
    for s in range(layers):
        trace = trace + jnp.where(row == col, k.new[z, s], 0.0)
    part = (1.0 + s_next) * trace - s_next * squares
    k.sums[...] = jnp.broadcast_to(jnp.sum(part, keepdims=True), k.sums.shape)
    put_row((k.near, k.far, k.side), k.sums[0:1, :])


def last_square_kernel(step, sums_at, closed, k):
    square_step(k, step, sums_at, closed)
    k.done[...] = jnp.zeros_like(k.done)


def gradient_edges(k, s_k, g, z, closed):
    slots, layers = g.shape[0], g.shape[1]

    def edge(i):
        i, s = i // layers, i % layers
        t = i + (i >= z).astype(jnp.int32)
        r, c, l = slot_offsets(k.off, t, layers)
        e, f = k.gs[t, s], k.xs[t, s]
        b = lax.rem(s + l, layers)
        product = edge_product(
            [k.g_cols[1 - c, s], k.x_cols[1 - c, s], e, f],
            [f, e, k.x_rows[1 + r, b], k.g_rows[1 + r, b]],
        )
        if closed:
            product = product + k.terms[t, s]
        k.new[t, s] = (1.0 + s_k) * g[t, s] - s_k * product

    each((slots - 1) * layers, edge, closed)


def gradient_terms(k, name, value):
    lefts = [(k.gs, k.g_near_a, k.g_near_b), (k.xs, k.x_near_a, k.x_near_b)]
    closed_terms(k, name, k.terms, value, lefts, lefts[::-1])


def gradient_tail(k, z, closed):
    layers = k.x.shape[1]
    for ref in (k.near, k.far, k.side):
        put_pairs(ref, 0, [k.new[z, s] for s in range(layers)])
    split_all(k.new, k.ns, closed)
    split_all(k.before, k.bs, closed)
    vertex_sums(k.off, k.ns, k.bs, k.acc, closed)
    send_sums(k.acc, 1, k.near, k.far, True)
    for s in range(layers):
        k.local[s] = symmetric(k.acc[1, s])
    if closed:
        closed_send(k, "out", k.new, k.ns, k.bs, True, 0, 1)


def first_gradient_kernel(step, four, closed, k):
    layers = k.x.shape[1]
    s_k = sign_of(k.branch, step)
    z = zero_slot(k.off, k.x.shape[0])
    split_all(k.h, k.gs, closed)
    split_all(k.x, k.xs, closed)
    own_h = [k.h[z, s] for s in range(layers)]
    diagonal_blocks(k, "h", own_h, k.g_rows, k.g_cols, 1)
    diagonal_blocks(k, "m", [k.x[z, s] for s in range(layers)], k.x_rows, k.x_cols, 0)
    cross = add_sums([k.h_local[s] for s in range(layers)], k.m_row_near, k.m_row_far, 2)
    for s in range(layers):
        k.new[z, s] = (1.0 + s_k) * own_h[s] - s_k * cross[s]
    if closed:
        closed_edges(k, "he", k.g_near_a, k.g_near_b, lambda ref, key, s: ref[2, s])
        closed_edges(k, "e", k.x_near_a, k.x_near_b, lambda ref, key, s: ref[1, s])
        gradient_terms(k, "e", lambda ref, key, s: ref[2, s])
    gradient_edges(k, s_k, k.h, z, closed)
    gradient_tail(k, z, closed)

    def weigh(i):
        t, s = i // layers, i % layers
        return ((1.0 + s_k) * k.h[t, s] + k.new[t, s]) * k.x[t, s]

    energy = total_of(k.x.shape[0] * layers, weigh, jnp.zeros_like(k.x[0, 0]), closed)
    k.sums[0:1, :] = row_sum(
        four, k.occupied[0:1, :], get_row(k.m_row_near), get_row(k.m_row_far), k.rest[0:1, :]
    )
    k.sums[1:2, :] = jnp.broadcast_to(0.5 * jnp.sum(energy, keepdims=True), (1, k.sums.shape[1]))
    k.sums[2:, :] = jnp.zeros_like(k.sums[2:, :])


def next_gradient_kernel(step, order, closed, k):
    slots, layers, size = k.x.shape[0], k.x.shape[1], k.x.shape[2]
    s_k = sign_of(k.branch, step)
    s_after = sign_of(k.branch, step + 1)
    sums = k.sums[...] + k.done[...]
    k.passed[...] = sums
    excess = sums[0:1, :] * (1.0 / order) - 0.5
    z = zero_slot(k.off, slots)
    row, col = iotas(size)
    eye = jnp.where(row == col, excess * (1.0 + s_after), 0.0)
    scale = excess * (-2.0 * s_after)

    def assemble(i):
        t, s = i // layers, i % layers
        k.g[t, s] = k.gh[t, s] + scale * k.after[t, s]

    each(slots * layers, assemble, closed)
    for s in range(layers):
        k.g[z, s] = k.g[z, s] + eye
    split_all(k.g, k.gs, closed)
    split_all(k.x, k.xs, closed)
    own_g = [k.g[z, s] for s in range(layers)]
    own_x = [k.x[z, s] for s in range(layers)]

    def blocks(message, pair):
        now, then = (unpack_pair(m[0, pair]) for m in message)
        return [a + scale * b + eye for a, b in zip(now, then)]

    gm, am = messages(k, "gm"), messages(k, "am")
    both = {side: (gm[side], am[side]) for side in SIDES}
    fill_neighbours(k.g_rows, own_g, both["row_near"], both["row_far"], odd("row"), blocks)
    fill_neighbours(k.g_cols, own_g, both["col_near"], both["col_far"], odd("col"), blocks)
    diagonal_blocks(k, "m", own_x, k.x_rows, k.x_cols, 0)
    own_sums = add_sums([k.g_local[s] for s in range(layers)], k.gm_row_near, k.gm_row_far, 1)
    cross_sums = add_sums([k.cross_local[s] for s in range(layers)], k.am_row_near, k.am_row_far, 3)
    twice = 2.0 * (1.0 + s_after) * excess
    for s in range(layers):
        cross = own_sums[s] + scale * cross_sums[s] + twice * own_x[s]
        k.new[z, s] = (1.0 + s_k) * own_g[s] - s_k * cross
    if closed:
        ae = messages(k, "ae")
        closed_edges(
            k, "ge", k.g_near_a, k.g_near_b, lambda ref, key, s: ref[1, s] + scale * ae[key][1, s]
        )
        closed_edges(k, "e", k.x_near_a, k.x_near_b, lambda ref, key, s: ref[1, s])
        gradient_terms(k, "ge", lambda ref, key, s: ref[0, s] + scale * ae[key][3, s])
    gradient_edges(k, s_k, k.g, z, closed)
    gradient_tail(k, z, closed)
    k.energy[...] = jnp.broadcast_to(sums[1:2, :], k.energy.shape)
    put_row((k.near, k.far, k.side), sums[1:2, :])


def last_gradient_kernel(step, order, four, closed, k):
    layers = k.x.shape[1]
    s_k = sign_of(k.branch, step)
    z = zero_slot(k.off, k.x.shape[0])
    split_all(k.g, k.gs, closed)
    split_all(k.x, k.xs, closed)
    own_g = [k.g[z, s] for s in range(layers)]
    diagonal_blocks(k, "gm", own_g, k.g_rows, k.g_cols, 0)
    diagonal_blocks(k, "m", [k.x[z, s] for s in range(layers)], k.x_rows, k.x_cols, 0)
    cross = add_sums([k.g_local[s] for s in range(layers)], k.gm_row_near, k.gm_row_far, 1)
    for s in range(layers):
        k.new[z, s] = (1.0 + s_k) * own_g[s] - s_k * cross[s]
    if closed:
        closed_edges(k, "ge", k.g_near_a, k.g_near_b, lambda ref, key, s: ref[1, s])
        closed_edges(k, "e", k.x_near_a, k.x_near_b, lambda ref, key, s: ref[1, s])
        gradient_terms(k, "ge", lambda ref, key, s: ref[0, s])
    gradient_edges(k, s_k, k.g, z, closed)
    energy = row_sum(four, k.energy[...], get_row(k.gm_row_near), get_row(k.gm_row_far), k.rest[...])
    lane = lax.broadcasted_iota(jnp.int32, k.totals.shape, 1)
    k.totals[...] = jnp.where(lane == 0, energy, k.sums[0:1, :]) * (1.0 / order)


def call(kernel, smem, vmem, outs, scratch, smem_outs=()):
    names = [*smem, *vmem, *outs, *dict(smem_outs), *scratch]
    small = dict(smem_outs)

    def body(*refs):
        kernel(types.SimpleNamespace(**dict(zip(names, refs))))

    results = pl.pallas_call(
        body,
        out_shape=[jax.ShapeDtypeStruct(shape, F32) for shape in outs.values()]
        + [jax.ShapeDtypeStruct(shape, jnp.int32) for shape in small.values()],
        in_specs=[pl.BlockSpec(memory_space=pltpu.SMEM)] * len(smem)
        + [pl.BlockSpec(memory_space=pltpu.VMEM)] * len(vmem),
        out_specs=[pl.BlockSpec(memory_space=pltpu.VMEM)] * len(outs)
        + [pl.BlockSpec(memory_space=pltpu.SMEM)] * len(small),
        scratch_shapes=list(scratch.values()),
        compiler_params=pltpu.CompilerParams(vmem_limit_bytes=40 * 1024 * 1024),
    )(*smem.values(), *vmem.values())
    return types.SimpleNamespace(**dict(zip([*outs, *small], results)))


def pairs_of(axis):
    count = lax.axis_size(axis)
    near = [(i, i ^ 1) for i in range(count)]
    far = [(i, (i - 1) % count if i % 2 == 0 else (i + 1) % count) for i in range(count)]
    return near, far


def swap(col_far, col_near, row_near, row_far):
    near_row, far_row = pairs_of("row")
    near_col, far_col = pairs_of("col")
    return dict(
        col_far=lax.ppermute(col_far, "col", far_col),
        col_near=lax.ppermute(col_near, "col", near_col),
        row_near=lax.ppermute(row_near, "row", near_row),
        row_far=lax.ppermute(row_far, "row", far_row),
    )


def exchange(k):
    return swap(k.side, k.side, k.near, k.far)


def exchange_edges(k):
    return swap(k.out_col_far, k.out_col_near, k.out_row_near, k.out_row_far)


def named(name, arrays):
    return {name + "_" + side: arrays[side] for side in SIDES}


def total_over(value, axis):
    count = lax.axis_size(axis)
    if count & (count - 1):
        return lax.psum(value, axis)
    step = 1
    while step < count:
        value = value + lax.ppermute(value, axis, [(i, i ^ step) for i in range(count)])
        step *= 2
    return value


def four_rows():
    return lax.axis_size("row") == 4


def row_remainder(value):
    if four_rows():
        return lax.ppermute(value, "row", [(i, i ^ 2) for i in range(4)])
    return total_over(value, "row")


def row_sum(four, own, near, far, rest):
    return (own + near) + (far + rest) if four else rest


class Shapes:
    def __init__(self, density):
        slots, layers, size = density.shape[2:5]
        self.full = (slots, layers, size, size)
        self.local = (layers, size, size)
        self.tile = (8, size)
        self.order = float(size * layers * lax.axis_size("row") * lax.axis_size("col"))
        self.split = pltpu.VMEM((slots, layers, size, 2 * size), BF16)
        self.three = pltpu.VMEM((3, layers, size, 2 * size), BF16)
        self.two = pltpu.VMEM((2, layers, size, 2 * size), BF16)
        self.two_wide = pltpu.VMEM((2, layers, size, size), F32)
        self.acc = pltpu.VMEM((3, layers, size, size), F32)
        self.wide = pltpu.VMEM(self.full, F32)
        self.pairs = (layers // 2, size + EXTRA, size)

    def messages(self, rows, cols):
        return dict(near=(rows, *self.pairs), far=(rows, *self.pairs), side=(cols, *self.pairs))

    def edges(self, count, closed):
        return {"out_" + side: (count, *self.local) for side in SIDES} if closed else {}

    def near_edges(self, names, closed):
        if not closed:
            return {}
        out = dict(terms=self.wide, came_a=self.two_wide, came_b=self.two_wide)
        for name in names:
            out[name + "_near_a"] = self.two
            out[name + "_near_b"] = self.two
        return out


def steps(closed, density, hamiltonian, table, branch, local0, near0):
    shape = Shapes(density)
    x0 = density.reshape(shape.full)
    h = hamiltonian.reshape(shape.full)
    full, local, tile, order = shape.full, shape.local, shape.tile, shape.order
    split, three, acc = shape.split, shape.three, shape.acc
    smem = dict(off=table, branch=branch)
    four = four_rows()
    square_scratch = dict(xs=split, x_rows=three, x_cols=three, **shape.near_edges(["x"], closed))
    pair_scratch = dict(
        gs=split, xs=split, g_rows=three, g_cols=three, x_rows=three, x_cols=three,
        **shape.near_edges(["g", "x"], closed),
    )
    tail = dict(ns=split, bs=split, acc=acc)

    def edges(**fields):
        out = {}
        for name, arrays in fields.items():
            out.update(named(name, arrays) if closed else {})
        return out

    edge0 = edge1 = edge2 = edge_gh = edge_g1 = None
    if closed:
        k = call(closed_start_kernel, dict(off=table), dict(x=x0, h=h), shape.edges(3, True), dict(xs=split))
        edge0 = exchange_edges(k)
    k = call(
        lambda k: square_kernel(0, 2, closed, k), smem,
        dict(x=x0, x_local=local0, **named("m", near0), **edges(e=edge0)),
        dict(new=full, local=local, **shape.messages(2, 1), **shape.edges(2, closed)),
        dict(ns=split, acc=acc, **square_scratch),
    )
    x1, local1, near1 = k.new, k.local, exchange(k)
    if closed:
        edge1 = exchange_edges(k)
    k = call(
        lambda k: turn_square_kernel(1, 1, closed, k), smem,
        dict(x=x1, x_local=local1, h=h, **named("m", near1), **edges(e=edge1)),
        dict(new=full, local=local, h_local=local, cross_local=local, sums=tile,
             **shape.messages(4, 1), **shape.edges(4, closed)),
        dict(ns=split, hs=split, acc=acc, acc_h=acc, acc_cross=acc, **square_scratch),
    )
    x2, local2, h_local, cross_local, occupied, near2 = (
        k.new, k.local, k.h_local, k.cross_local, k.sums, exchange(k)
    )
    if closed:
        edge2 = exchange_edges(k)
    rest = row_remainder(occupied)
    k = call(
        lambda k: first_gradient_kernel(2, four, closed, k), smem,
        dict(h=h, x=x2, before=x1, h_local=h_local, **named("h", near0), **named("m", near2),
             occupied=occupied, rest=rest, **edges(he=edge0, e=edge2)),
        dict(new=full, local=local, sums=tile, **shape.messages(2, 1), **shape.edges(2, closed)),
        dict(**pair_scratch, **tail),
    )
    gh, gh_local, sums, near_gh = k.new, k.local, k.sums, exchange(k)
    if closed:
        edge_gh = exchange_edges(k)
    sums = total_over(sums, "col")
    k = call(
        lambda k: last_square_kernel(2, 1, closed, k), smem,
        dict(**named("m", near2), x=x2, x_local=local2, **edges(e=edge2)),
        dict(new=full, done=tile), square_scratch,
    )
    x3, done = k.new, k.done
    k = call(
        lambda k: next_gradient_kernel(1, order, closed, k), smem,
        dict(sums=sums, done=done, gh=gh, after=x2, x=x1, before=x0, g_local=gh_local,
             cross_local=cross_local, **named("gm", near_gh), **named("am", near2), **named("m", near1),
             **edges(ge=edge_gh, ae=edge2, e=edge1)),
        dict(new=full, local=local, passed=tile, energy=tile,
             **shape.messages(2, 1), **shape.edges(2, closed)),
        dict(g=shape.wide, **pair_scratch, **tail),
    )
    g1, g1_local, sums, energy, near_g1 = k.new, k.local, k.passed, k.energy, exchange(k)
    if closed:
        edge_g1 = exchange_edges(k)
    rest = row_remainder(energy)
    k = call(
        lambda k: last_gradient_kernel(0, order, four, closed, k), smem,
        dict(sums=sums, energy=energy, rest=rest, g=g1, x=x0, g_local=g1_local,
             **named("gm", near_g1), **named("m", near0), **edges(ge=edge_g1, e=edge0)),
        dict(new=full, totals=tile), pair_scratch,
    )
    return x3.reshape(density.shape), k.new.reshape(density.shape), k.totals[0, :2]


def local(density, hamiltonian, offsets, branch):
    shape = Shapes(density)
    x0 = density.reshape(shape.full)
    h = hamiltonian.reshape(shape.full)
    rows, cols = lax.axis_size("row"), lax.axis_size("col")
    k = call(
        lambda k: start_kernel(rows, cols, k), dict(off=offsets), dict(x=x0, h=h),
        dict(local=shape.local, **shape.messages(3, 2)), dict(xs=shape.split, acc=shape.acc),
        dict(flag=(1,), table=offsets.shape),
    )
    near0 = exchange(k)
    return lax.cond(
        k.flag[0] > 0, lambda *a: steps(True, *a), lambda *a: steps(False, *a),
        density, hamiltonian, k.table, branch, k.local, near0,
    )


def solution(mesh):
    return jax.shard_map(
        local,
        mesh=mesh,
        in_specs=(
            P("row", "col", None, None, None, None),
            P("row", "col", None, None, None, None),
            P(),
            P(),
        ),
        out_specs=(
            P("row", "col", None, None, None, None),
            P("row", "col", None, None, None, None),
            P(),
        ),
        check_vma=False,
    )
```

```python
import types

import jax
import jax.numpy as jnp
from jax import lax
from jax.experimental import pallas as pl
from jax.experimental.pallas import tpu as pltpu
from jax.sharding import PartitionSpec as P

F32 = jnp.float32
BF16 = jnp.bfloat16
EXTRA = 8
SIDES = ("col_far", "col_near", "row_near", "row_far")


def each(count, body, rolled):
    if not rolled:
        for i in range(count):
            body(i)
        return

    def step(i, carry):
        body(i)
        return carry

    lax.fori_loop(0, count, step, 0)


def total_of(count, term, first, rolled):
    if not rolled:
        for i in range(count):
            first = first + term(i)
        return first
    return lax.fori_loop(0, count, lambda i, sum_: sum_ + term(i), first)


def iotas(size):
    shape = (size, size)
    return lax.broadcasted_iota(jnp.int32, shape, 0), lax.broadcasted_iota(jnp.int32, shape, 1)


def store_split(dst, index, value):
    size = value.shape[-1]
    high = value.astype(BF16)
    dst[index + (slice(None), slice(0, size))] = high
    dst[index + (slice(None), slice(size, 2 * size))] = (value - high.astype(F32)).astype(BF16)


def split_all(src, dst, rolled):
    layers = src.shape[1]

    def one(i):
        t, s = i // layers, i % layers
        store_split(dst, (t, s), src[t, s])

    each(src.shape[0] * layers, one, rolled)


def quadrants(q):
    size = q.shape[-1] // 2
    return (q[:size, :size] + q[size:, size:]) + (q[:size, size:] + q[size:, :size])


def edge_product(lefts, rights):
    size = lefts[0].shape[0]
    high = [x[:, :size] for x in lefts]
    low = [x[:, size:] for x in lefts]
    lhs = jnp.concatenate([jnp.concatenate(high, 1), jnp.concatenate(low, 1)], 0)
    rhs = jnp.concatenate(rights, 0)
    return quadrants(jnp.dot(lhs, rhs, preferred_element_type=F32))


def turned(value):
    size = value.shape[0]
    parts = [value[:, :size], value[:, size:]]
    return jnp.concatenate([x.astype(F32).T.astype(BF16) for x in parts], 1)


def symmetric(value):
    return value + value.T


def pack_pair(first, second):
    size = first.shape[-1]
    row, col = iotas(size)
    body = jnp.where(row <= col, first, second)
    diagonal = jnp.sum(jnp.where(row == col, second, 0.0), axis=0, keepdims=True)
    return jnp.concatenate([body, jnp.broadcast_to(diagonal, (EXTRA, size))], axis=0)


def unpack_pair(packed):
    size = packed.shape[-1]
    row, col = iotas(size)
    body = packed[:size]
    other = body.T
    second_diagonal = packed[size : size + 1]
    first = jnp.where(row <= col, body, other)
    second = jnp.where(row > col, body, jnp.where(row == col, second_diagonal, other))
    return first, second


def put_pairs(ref, which, blocks):
    for k in range(len(blocks) // 2):
        ref[which, k] = pack_pair(blocks[2 * k], blocks[2 * k + 1])


def put_row(refs, value):
    size = value.shape[-1]
    for ref in refs:
        ref[0, 0, size + 1 : size + 2, :] = value


def get_row(ref):
    size = ref.shape[-1]
    return ref[0, 0, size + 1 : size + 2, :]


def odd(axis):
    return lax.rem(lax.axis_index(axis), 2)


def wrap(layer, layers):
    return lax.rem(layer + 2 * layers, layers)


def slot_offsets(off, t, layers):
    return off[t, 0], off[t, 1], lax.rem(off[t, 2] + layers, layers)


def zero_slot(off, slots):
    z = jnp.int32(0)
    for t in range(slots):
        hit = (off[t, 0] == 0) & (off[t, 1] == 0) & (off[t, 2] == 0)
        z = jnp.where(hit, jnp.int32(t), z)
    return z


def sign_of(branch, k):
    return (2 * branch[k] - 1).astype(F32)


def closes(off, slots, layers, rows, cols):
    def code(r, c, l):
        return (r + 1) * (3 * layers) + (c + 1) * layers + l

    held = jnp.int32(0)
    places = []
    for t in range(slots):
        r, c, l = slot_offsets(off, t, layers)
        nonzero = (r != 0) | (c != 0) | (l != 0)
        held = held | jnp.where(nonzero, jnp.left_shift(jnp.int32(1), code(r, c, l)), 0)
        places.append((r, c, l, nonzero))
    found = jnp.int32(0)
    for i in range(slots):
        for j in range(i + 1):
            (r, c, l, some), (r2, c2, l2, some2) = places[i], places[j]
            r3 = lax.rem(r + r2 + 1 + rows, rows) - 1
            c3 = lax.rem(c + c2 + 1 + cols, cols) - 1
            l3 = lax.rem(l + l2, layers)
            inside = (r3 <= 1) & (c3 <= 1) & some & some2
            place = jnp.where(inside, code(r3, c3, l3), 0)
            hit = jnp.right_shift(held, place) & 1
            found = found | jnp.where(inside, hit, 0)
    return found


def triangle(off, slots, layers):
    def find(test):
        place = jnp.int32(0)
        for t in range(slots):
            place = jnp.where(test(off[t, 0], off[t, 1]), jnp.int32(t), place)
        return place

    g = types.SimpleNamespace()
    g.a = [find(lambda r, c, d=d: (r == d) & (c == 0)) for d in (-1, 1)]
    g.c = [find(lambda r, c, d=d: (r == d) & (c != 0)) for d in (-1, 1)]
    g.beta = off[g.c[1], 1]
    g.b = [find(lambda r, c, d=d: (r == 0) & (c == d * g.beta)) for d in (-1, 1)]
    g.la, g.lb, g.lc = (lax.rem(off[x[1], 2] + layers, layers) for x in (g.a, g.b, g.c))
    return g


def pick(pair, index):
    return jnp.where(index > 0, pair[1], pair[0])


def vertex_sums(off, left, right, acc, rolled):
    slots, layers = left.shape[0], left.shape[1]
    acc[...] = jnp.zeros_like(acc)

    def add(i):
        t, s = i // layers, i % layers
        r, _, l = slot_offsets(off, t, layers)
        q = lax.dot_general(
            left[t, s], right[t, s], (((0,), (0,)), ((), ())), preferred_element_type=F32
        )
        acc[r + 1, lax.rem(s + l, layers)] += quadrants(q)

    each(slots * layers, add, rolled)


def send_sums(acc, which, near, far, sym):
    layers = acc.shape[1]
    parity = odd("row")
    for r, ref in ((2 - 2 * parity, near), (2 * parity, far)):
        blocks = [acc[r, s] for s in range(layers)]
        put_pairs(ref, which, [symmetric(b) for b in blocks] if sym else blocks)


def add_sums(value, near, far, which):
    out = list(value)
    for k in range(len(out) // 2):
        for message in (near, far):
            first, second = unpack_pair(message[which, k])
            out[2 * k] = out[2 * k] + first
            out[2 * k + 1] = out[2 * k + 1] + second
    return out


def fill_neighbours(dst, own, near, far, parity, blocks):
    for k in range(dst.shape[1] // 2):
        for slot, message in ((2 - 2 * parity, near), (2 * parity, far)):
            first, second = blocks(message, k)
            store_split(dst, (slot, 2 * k), first)
            store_split(dst, (slot, 2 * k + 1), second)
    for s in range(dst.shape[1]):
        store_split(dst, (1, s), own[s])


def diagonal_blocks(k, name, own, rows, cols, which):
    def blocks(message, pair):
        return unpack_pair(message[which, pair])

    side = messages(k, name)
    fill_neighbours(rows, own, side["row_near"], side["row_far"], odd("row"), blocks)
    fill_neighbours(cols, own, side["col_near"], side["col_far"], odd("col"), blocks)


def messages(k, name):
    return {side: getattr(k, name + "_" + side) for side in SIDES}


def closed_send(k, out, f32, left, right, cross, sums_at, edges_at):
    slots, layers = left.shape[0], left.shape[1]
    g = triangle(k.off, slots, layers)
    side = messages(k, out)

    def two(x, y):
        lefts, rights = x(left), y(right)
        if not cross:
            return edge_product([lefts], [rights])
        return edge_product([lefts, x(right)], [rights, y(left)])

    parity = odd("row")
    for index, ref in ((1 - parity, side["row_near"]), (parity, side["row_far"])):
        d = 2 * index - 1
        b, c, other = pick(g.b, index), pick(g.c, index), pick(g.b, 1 - index)

        def row_blocks(s, ref=ref, d=d, b=b, c=c, other=other):
            m = wrap(s - d * g.lc, layers)
            if sums_at is not None:
                ref[sums_at, s] = two(lambda x: turned(x[c, m]), lambda x: x[b, m])
            if edges_at is not None:
                ref[edges_at, s] = f32[other, s]

        each(layers, row_blocks, True)
    parity = odd("col")
    for d, ref in ((1 - 2 * parity, side["col_near"]), (2 * parity - 1, side["col_far"])):
        sigma = d * g.beta
        index = (sigma + 1) // 2
        a, other, c = pick(g.a, index), pick(g.a, 1 - index), pick(g.c, 1 - index)

        def col_blocks(s, ref=ref, sigma=sigma, a=a, other=other, c=c):
            m = wrap(s + sigma * g.lb, layers)
            if sums_at is not None:
                ref[sums_at, s] = two(lambda x: x[other, s], lambda x: turned(x[c, m]))
            if edges_at is not None:
                ref[edges_at, s] = f32[a, s]

        each(layers, col_blocks, True)


def closed_edges(k, name, near_a, near_b, value):
    layers = near_a.shape[1]
    g = triangle(k.off, k.off.shape[0], layers)
    side = messages(k, name)
    parity = odd("row")
    for index, key in ((1 - parity, "row_near"), (parity, "row_far")):
        each(
            layers,
            lambda s, i=index, key=key: store_split(near_b, (i, s), value(side[key], key, s)),
            True,
        )
    parity = odd("col")
    for d, key in ((1 - 2 * parity, "col_near"), (2 * parity - 1, "col_far")):
        index = (1 - d * g.beta) // 2
        each(
            layers,
            lambda s, i=index, key=key: store_split(near_a, (i, s), value(side[key], key, s)),
            True,
        )


def closed_terms(k, name, terms, value, lefts, rights):
    layers = terms.shape[1]
    g = triangle(k.off, k.off.shape[0], layers)
    side = messages(k, name)
    parity = odd("row")
    for index, key in ((1 - parity, "row_near"), (parity, "row_far")):
        for s in range(layers):
            k.came_a[index, s] = value(side[key], key, s)
    parity = odd("col")
    for d, key in ((1 - 2 * parity, "col_near"), (2 * parity - 1, "col_far")):
        index = (1 - d * g.beta) // 2
        for s in range(layers):
            k.came_b[index, s] = value(side[key], key, s)

    def product(x, y):
        return edge_product([x(*left) for left in lefts], [y(*right) for right in rights])

    def corner(i):
        index, s = i // layers, i % layers
        sigma = 2 * index - 1
        a, b, c = pick(g.a, index), pick(g.b, index), pick(g.c, index)
        back, on, up = (wrap(s + m, layers) for m in (-sigma * g.lb, sigma * g.lb, sigma * g.la))
        terms[a, s] = k.came_a[index, s] + product(
            lambda f, ea, eb: turned(f[b, back]), lambda f, ea, eb: f[c, back]
        )
        terms[b, s] = k.came_b[index, s] + product(
            lambda f, ea, eb: f[c, s], lambda f, ea, eb: turned(f[a, on])
        )
        terms[c, s] = product(lambda f, ea, eb: f[b, s], lambda f, ea, eb: f[a, on]) + product(
            lambda f, ea, eb: ea[index, s], lambda f, ea, eb: eb[index, up]
        )

    each(2 * layers, corner, True)


def start_kernel(rows, cols, k):
    slots, layers = k.x.shape[0], k.x.shape[1]
    z = zero_slot(k.off, slots)
    for t in range(slots):
        for j in range(3):
            k.table[t, j] = k.off[t, j]
    k.flag[0] = closes(k.off, slots, layers, rows, cols)
    split_all(k.x, k.xs, False)
    vertex_sums(k.off, k.xs, k.xs, k.acc, False)
    for ref in (k.near, k.far, k.side):
        put_pairs(ref, 0, [k.x[z, s] for s in range(layers)])
        put_pairs(ref, 1, [k.h[z, s] for s in range(layers)])
    send_sums(k.acc, 2, k.near, k.far, False)
    for s in range(layers):
        k.local[s] = k.acc[1, s]


def closed_start_kernel(k):
    split_all(k.x, k.xs, True)
    closed_send(k, "out", k.x, k.xs, k.xs, False, 0, 1)
    closed_send(k, "out", k.h, k.xs, k.xs, False, None, 2)


def square_step(k, step, sums_at, closed):
    slots, layers = k.x.shape[0], k.x.shape[1]
    s_k = sign_of(k.branch, step)
    z = zero_slot(k.off, slots)
    split_all(k.x, k.xs, closed)
    own = [k.x[z, s] for s in range(layers)]
    diagonal_blocks(k, "m", own, k.x_rows, k.x_cols, 0)
    square = add_sums([k.x_local[s] for s in range(layers)], k.m_row_near, k.m_row_far, sums_at)
    for s in range(layers):
        k.new[z, s] = own[s] + s_k * (own[s] - square[s])
    if closed:
        closed_edges(k, "e", k.x_near_a, k.x_near_b, lambda ref, key, s: ref[1, s])
        operand = [(k.xs, k.x_near_a, k.x_near_b)]
        closed_terms(k, "e", k.terms, lambda ref, key, s: ref[0, s], operand, operand)

    def edge(i):
        i, s = i // layers, i % layers
        t = i + (i >= z).astype(jnp.int32)
        r, c, l = slot_offsets(k.off, t, layers)
        e = k.xs[t, s]
        product = edge_product([k.x_cols[1 - c, s], e], [e, k.x_rows[1 + r, lax.rem(s + l, layers)]])
        if closed:
            product = product + k.terms[t, s]
        e32 = k.x[t, s]
        k.new[t, s] = e32 + s_k * (e32 - product)

    each((slots - 1) * layers, edge, closed)
    return z


def square_kernel(step, sums_at, closed, k):
    layers = k.x.shape[1]
    z = square_step(k, step, sums_at, closed)
    for ref in (k.near, k.far, k.side):
        put_pairs(ref, 0, [k.new[z, s] for s in range(layers)])
    split_all(k.new, k.ns, closed)
    vertex_sums(k.off, k.ns, k.ns, k.acc, closed)
    send_sums(k.acc, 1, k.near, k.far, False)
    for s in range(layers):
        k.local[s] = k.acc[1, s]
    if closed:
        closed_send(k, "out", k.new, k.ns, k.ns, False, 0, 1)


def turn_square_kernel(step, sums_at, closed, k):
    square_kernel(step, sums_at, closed, k)
    slots, layers, size = k.x.shape[0], k.x.shape[1], k.x.shape[2]
    z = zero_slot(k.off, slots)
    split_all(k.h, k.hs, closed)
    vertex_sums(k.off, k.hs, k.ns, k.acc_h, closed)
    send_sums(k.acc_h, 2, k.near, k.far, True)
    vertex_sums(k.off, k.ns, k.xs, k.acc_cross, closed)
    send_sums(k.acc_cross, 3, k.near, k.far, True)
    for s in range(layers):
        k.h_local[s] = symmetric(k.acc_h[1, s])
        k.cross_local[s] = symmetric(k.acc_cross[1, s])
    if closed:
        closed_send(k, "out", None, k.hs, k.ns, True, 2, None)
        closed_send(k, "out", None, k.ns, k.xs, True, 3, None)
    s_next = sign_of(k.branch, step + 1)
    row, col = iotas(size)
    squares = total_of(
        slots * layers,
        lambda i: k.new[i // layers, i % layers] * k.new[i // layers, i % layers],
        jnp.zeros((size, size), F32),
        closed,
    )
    trace = jnp.zeros_like(squares)
    for s in range(layers):
        trace = trace + jnp.where(row == col, k.new[z, s], 0.0)
    part = (1.0 + s_next) * trace - s_next * squares
    k.sums[...] = jnp.broadcast_to(jnp.sum(part, keepdims=True), k.sums.shape)
    put_row((k.near, k.far, k.side), k.sums[0:1, :])


def last_square_kernel(step, sums_at, closed, k):
    square_step(k, step, sums_at, closed)
    k.done[...] = jnp.zeros_like(k.done)


def gradient_edges(k, s_k, g, z, closed):
    slots, layers = g.shape[0], g.shape[1]

    def edge(i):
        i, s = i // layers, i % layers
        t = i + (i >= z).astype(jnp.int32)
        r, c, l = slot_offsets(k.off, t, layers)
        e, f = k.gs[t, s], k.xs[t, s]
        b = lax.rem(s + l, layers)
        product = edge_product(
            [k.g_cols[1 - c, s], k.x_cols[1 - c, s], e, f],
            [f, e, k.x_rows[1 + r, b], k.g_rows[1 + r, b]],
        )
        if closed:
            product = product + k.terms[t, s]
        k.new[t, s] = (1.0 + s_k) * g[t, s] - s_k * product

    each((slots - 1) * layers, edge, closed)


def gradient_terms(k, name, value):
    lefts = [(k.gs, k.g_near_a, k.g_near_b), (k.xs, k.x_near_a, k.x_near_b)]
    closed_terms(k, name, k.terms, value, lefts, lefts[::-1])


def gradient_tail(k, z, closed):
    layers = k.x.shape[1]
    for ref in (k.near, k.far, k.side):
        put_pairs(ref, 0, [k.new[z, s] for s in range(layers)])
    split_all(k.new, k.ns, closed)
    split_all(k.before, k.bs, closed)
    vertex_sums(k.off, k.ns, k.bs, k.acc, closed)
    send_sums(k.acc, 1, k.near, k.far, True)
    for s in range(layers):
        k.local[s] = symmetric(k.acc[1, s])
    if closed:
        closed_send(k, "out", k.new, k.ns, k.bs, True, 0, 1)


def first_gradient_kernel(step, closed, k):
    layers = k.x.shape[1]
    s_k = sign_of(k.branch, step)
    z = zero_slot(k.off, k.x.shape[0])
    split_all(k.h, k.gs, closed)
    split_all(k.x, k.xs, closed)
    own_h = [k.h[z, s] for s in range(layers)]
    diagonal_blocks(k, "h", own_h, k.g_rows, k.g_cols, 1)
    diagonal_blocks(k, "m", [k.x[z, s] for s in range(layers)], k.x_rows, k.x_cols, 0)
    cross = add_sums([k.h_local[s] for s in range(layers)], k.m_row_near, k.m_row_far, 2)
    for s in range(layers):
        k.new[z, s] = (1.0 + s_k) * own_h[s] - s_k * cross[s]
    if closed:
        closed_edges(k, "he", k.g_near_a, k.g_near_b, lambda ref, key, s: ref[2, s])
        closed_edges(k, "e", k.x_near_a, k.x_near_b, lambda ref, key, s: ref[1, s])
        gradient_terms(k, "e", lambda ref, key, s: ref[2, s])
    gradient_edges(k, s_k, k.h, z, closed)
    gradient_tail(k, z, closed)

    def weigh(i):
        t, s = i // layers, i % layers
        return ((1.0 + s_k) * k.h[t, s] + k.new[t, s]) * k.x[t, s]

    energy = total_of(k.x.shape[0] * layers, weigh, jnp.zeros_like(k.x[0, 0]), closed)
    k.energy[...] = jnp.broadcast_to(0.5 * jnp.sum(energy, keepdims=True), k.energy.shape)


def next_gradient_kernel(step, order, closed, k):
    slots, layers, size = k.x.shape[0], k.x.shape[1], k.x.shape[2]
    s_k = sign_of(k.branch, step)
    s_after = sign_of(k.branch, step + 1)
    sums = k.sums[...] + k.done[...]
    excess = sums[0:1, :] * (1.0 / order) - 0.5
    z = zero_slot(k.off, slots)
    row, col = iotas(size)
    eye = jnp.where(row == col, excess * (1.0 + s_after), 0.0)
    scale = excess * (-2.0 * s_after)

    def assemble(i):
        t, s = i // layers, i % layers
        k.g[t, s] = k.gh[t, s] + scale * k.after[t, s]

    each(slots * layers, assemble, closed)
    for s in range(layers):
        k.g[z, s] = k.g[z, s] + eye
    split_all(k.g, k.gs, closed)
    split_all(k.x, k.xs, closed)
    own_g = [k.g[z, s] for s in range(layers)]
    own_x = [k.x[z, s] for s in range(layers)]

    def blocks(message, pair):
        now, then = (unpack_pair(m[0, pair]) for m in message)
        return [a + scale * b + eye for a, b in zip(now, then)]

    gm, am = messages(k, "gm"), messages(k, "am")
    both = {side: (gm[side], am[side]) for side in SIDES}
    fill_neighbours(k.g_rows, own_g, both["row_near"], both["row_far"], odd("row"), blocks)
    fill_neighbours(k.g_cols, own_g, both["col_near"], both["col_far"], odd("col"), blocks)
    diagonal_blocks(k, "m", own_x, k.x_rows, k.x_cols, 0)
    own_sums = add_sums([k.g_local[s] for s in range(layers)], k.gm_row_near, k.gm_row_far, 1)
    cross_sums = add_sums([k.cross_local[s] for s in range(layers)], k.am_row_near, k.am_row_far, 3)
    twice = 2.0 * (1.0 + s_after) * excess
    for s in range(layers):
        cross = own_sums[s] + scale * cross_sums[s] + twice * own_x[s]
        k.new[z, s] = (1.0 + s_k) * own_g[s] - s_k * cross
    if closed:
        ae = messages(k, "ae")
        closed_edges(
            k, "ge", k.g_near_a, k.g_near_b, lambda ref, key, s: ref[1, s] + scale * ae[key][1, s]
        )
        closed_edges(k, "e", k.x_near_a, k.x_near_b, lambda ref, key, s: ref[1, s])
        gradient_terms(k, "ge", lambda ref, key, s: ref[0, s] + scale * ae[key][3, s])
    gradient_edges(k, s_k, k.g, z, closed)
    gradient_tail(k, z, closed)
    k.energy[...] = jnp.broadcast_to(sums[1:2, :], k.energy.shape)
    put_row((k.near, k.far, k.side), sums[1:2, :])


def last_gradient_kernel(step, closed, k):
    layers = k.x.shape[1]
    s_k = sign_of(k.branch, step)
    z = zero_slot(k.off, k.x.shape[0])
    split_all(k.g, k.gs, closed)
    split_all(k.x, k.xs, closed)
    own_g = [k.g[z, s] for s in range(layers)]
    diagonal_blocks(k, "gm", own_g, k.g_rows, k.g_cols, 0)
    diagonal_blocks(k, "m", [k.x[z, s] for s in range(layers)], k.x_rows, k.x_cols, 0)
    cross = add_sums([k.g_local[s] for s in range(layers)], k.gm_row_near, k.gm_row_far, 1)
    for s in range(layers):
        k.new[z, s] = (1.0 + s_k) * own_g[s] - s_k * cross[s]
    if closed:
        closed_edges(k, "ge", k.g_near_a, k.g_near_b, lambda ref, key, s: ref[1, s])
        closed_edges(k, "e", k.x_near_a, k.x_near_b, lambda ref, key, s: ref[1, s])
        gradient_terms(k, "ge", lambda ref, key, s: ref[0, s])
    gradient_edges(k, s_k, k.g, z, closed)


def call(kernel, smem, vmem, outs, scratch, smem_outs=()):
    names = [*smem, *vmem, *outs, *dict(smem_outs), *scratch]
    small = dict(smem_outs)

    def body(*refs):
        kernel(types.SimpleNamespace(**dict(zip(names, refs))))

    results = pl.pallas_call(
        body,
        out_shape=[jax.ShapeDtypeStruct(shape, F32) for shape in outs.values()]
        + [jax.ShapeDtypeStruct(shape, jnp.int32) for shape in small.values()],
        in_specs=[pl.BlockSpec(memory_space=pltpu.SMEM)] * len(smem)
        + [pl.BlockSpec(memory_space=pltpu.VMEM)] * len(vmem),
        out_specs=[pl.BlockSpec(memory_space=pltpu.VMEM)] * len(outs)
        + [pl.BlockSpec(memory_space=pltpu.SMEM)] * len(small),
        scratch_shapes=list(scratch.values()),
        compiler_params=pltpu.CompilerParams(vmem_limit_bytes=40 * 1024 * 1024),
        cost_estimate=pl.CostEstimate(flops=2_000_000_000, bytes_accessed=6_000_000, transcendentals=0),
    )(*smem.values(), *vmem.values())
    return types.SimpleNamespace(**dict(zip([*outs, *small], results)))


def pairs_of(axis):
    count = lax.axis_size(axis)
    near = [(i, i ^ 1) for i in range(count)]
    far = [(i, (i - 1) % count if i % 2 == 0 else (i + 1) % count) for i in range(count)]
    return near, far


def swap(col_far, col_near, row_near, row_far):
    near_row, far_row = pairs_of("row")
    near_col, far_col = pairs_of("col")
    return dict(
        col_far=lax.ppermute(col_far, "col", far_col),
        col_near=lax.ppermute(col_near, "col", near_col),
        row_near=lax.ppermute(row_near, "row", near_row),
        row_far=lax.ppermute(row_far, "row", far_row),
    )


def exchange(k):
    out = swap(k.side, k.side, k.near, k.far)
    out["first"] = out["row_far"][0, 0, -EXTRA:, :] + out["col_far"][0, 0, -EXTRA:, :]
    return out


def exchange_edges(k):
    return swap(k.out_col_far, k.out_col_near, k.out_row_near, k.out_row_far)


def named(name, arrays):
    return {name + "_" + side: arrays[side] for side in SIDES}


def doubling(value, axis, steps):
    for step in steps:
        count = lax.axis_size(axis)
        value = value + lax.ppermute(value, axis, [(i, i ^ step) for i in range(count)])
    return value


def powers(axis):
    count = lax.axis_size(axis)
    return [] if count & (count - 1) else [1 << i for i in range(count.bit_length() - 1)]


def col_first(value):
    steps = powers("col")
    return doubling(value, "col", steps[:1]) if steps else lax.psum(value, "col")


def col_rest(value):
    return doubling(value, "col", powers("col")[1:])


def row_total(value, came):
    if lax.axis_size("row") == 4:
        rest = lax.ppermute(value, "row", [(i, i ^ 2) for i in range(4)])
        row = value.shape[-1] + 1
        near, far = (came[side][0, 0, row : row + 1] for side in ("row_near", "row_far"))
        return (value + near) + (far + rest)
    steps = powers("row")
    return doubling(value, "row", steps) if steps else lax.psum(value, "row")


class Shapes:
    def __init__(self, density):
        slots, layers, size = density.shape[2:5]
        self.full = (slots, layers, size, size)
        self.local = (layers, size, size)
        self.tile = (8, size)
        self.order = float(size * layers * lax.axis_size("row") * lax.axis_size("col"))
        self.split = pltpu.VMEM((slots, layers, size, 2 * size), BF16)
        self.three = pltpu.VMEM((3, layers, size, 2 * size), BF16)
        self.two = pltpu.VMEM((2, layers, size, 2 * size), BF16)
        self.two_wide = pltpu.VMEM((2, layers, size, size), F32)
        self.acc = pltpu.VMEM((3, layers, size, size), F32)
        self.wide = pltpu.VMEM(self.full, F32)
        self.pairs = (layers // 2, size + EXTRA, size)

    def messages(self, rows, cols):
        return dict(near=(rows, *self.pairs), far=(rows, *self.pairs), side=(cols, *self.pairs))

    def edges(self, count, closed):
        return {"out_" + side: (count, *self.local) for side in SIDES} if closed else {}

    def near_edges(self, names, closed):
        if not closed:
            return {}
        out = dict(terms=self.wide, came_a=self.two_wide, came_b=self.two_wide)
        for name in names:
            out[name + "_near_a"] = self.two
            out[name + "_near_b"] = self.two
        return out


def steps(closed, density, hamiltonian, table, branch, local0, near0):
    shape = Shapes(density)
    x0 = density.reshape(shape.full)
    h = hamiltonian.reshape(shape.full)
    full, local, tile, order = shape.full, shape.local, shape.tile, shape.order
    split, three, acc = shape.split, shape.three, shape.acc
    smem = dict(off=table, branch=branch)
    square_scratch = dict(xs=split, x_rows=three, x_cols=three, **shape.near_edges(["x"], closed))
    pair_scratch = dict(
        gs=split, xs=split, g_rows=three, g_cols=three, x_rows=three, x_cols=three,
        **shape.near_edges(["g", "x"], closed),
    )
    tail = dict(ns=split, bs=split, acc=acc)

    def edges(**fields):
        out = {}
        for name, arrays in fields.items():
            out.update(named(name, arrays) if closed else {})
        return out

    edge0 = edge1 = edge2 = edge_gh = edge_g1 = None
    if closed:
        k = call(closed_start_kernel, dict(off=table), dict(x=x0, h=h), shape.edges(3, True), dict(xs=split))
        edge0 = exchange_edges(k)
    k = call(
        lambda k: square_kernel(0, 2, closed, k), smem,
        dict(x=x0, x_local=local0, first=near0["first"], **named("m", near0), **edges(e=edge0)),
        dict(new=full, local=local, **shape.messages(2, 1), **shape.edges(2, closed)),
        dict(ns=split, acc=acc, **square_scratch),
    )
    x1, local1, near1 = k.new, k.local, exchange(k)
    if closed:
        edge1 = exchange_edges(k)
    k = call(
        lambda k: turn_square_kernel(1, 1, closed, k), smem,
        dict(x=x1, x_local=local1, h=h, first=near1["first"], **named("m", near1), **edges(e=edge1)),
        dict(new=full, local=local, h_local=local, cross_local=local, sums=tile,
             **shape.messages(4, 1), **shape.edges(4, closed)),
        dict(ns=split, hs=split, acc=acc, acc_h=acc, acc_cross=acc, **square_scratch),
    )
    x2, local2, h_local, cross_local, occupied, near2 = (
        k.new, k.local, k.h_local, k.cross_local, k.sums, exchange(k)
    )
    if closed:
        edge2 = exchange_edges(k)
    occupied = col_first(row_total(occupied, near2))
    k = call(
        lambda k: first_gradient_kernel(2, closed, k), smem,
        dict(h=h, x=x2, before=x1, h_local=h_local, first=near2["first"], **named("h", near0), **named("m", near2),
             **edges(he=edge0, e=edge2)),
        dict(new=full, local=local, energy=tile, **shape.messages(2, 1), **shape.edges(2, closed)),
        dict(**pair_scratch, **tail),
    )
    gh, gh_local, energy, near_gh = k.new, k.local, k.energy, exchange(k)
    if closed:
        edge_gh = exchange_edges(k)
    row = lax.broadcasted_iota(jnp.int32, tile, 0)
    sums = col_rest(jnp.where(row == 0, occupied, energy))
    k = call(
        lambda k: last_square_kernel(2, 1, closed, k), smem,
        dict(**named("m", near2), x=x2, x_local=local2, **edges(e=edge2)),
        dict(new=full, done=tile), square_scratch,
    )
    x3, done = k.new, k.done
    k = call(
        lambda k: next_gradient_kernel(1, order, closed, k), smem,
        dict(sums=sums, done=done, first=near_gh["first"], gh=gh, after=x2, x=x1, before=x0, g_local=gh_local,
             cross_local=cross_local, **named("gm", near_gh), **named("am", near2), **named("m", near1),
             **edges(ge=edge_gh, ae=edge2, e=edge1)),
        dict(new=full, local=local, energy=tile,
             **shape.messages(2, 1), **shape.edges(2, closed)),
        dict(g=shape.wide, **pair_scratch, **tail),
    )
    g1, g1_local, energy, near_g1 = k.new, k.local, k.energy, exchange(k)
    if closed:
        edge_g1 = exchange_edges(k)
    energy = col_first(row_total(energy, near_g1))
    k = call(
        lambda k: last_gradient_kernel(0, closed, k), smem,
        dict(g=g1, x=x0, g_local=g1_local, first=near_g1["first"], **named("gm", near_g1), **named("m", near0),
             **edges(ge=edge_g1, e=edge0)),
        dict(new=full), pair_scratch,
    )
    lane = lax.broadcasted_iota(jnp.int32, (2,), 0)
    totals = jnp.where(lane == 0, energy[0, :2], sums[0, :2]) / order
    return x3.reshape(density.shape), k.new.reshape(density.shape), totals


def local(density, hamiltonian, offsets, branch):
    shape = Shapes(density)
    x0 = density.reshape(shape.full)
    h = hamiltonian.reshape(shape.full)
    rows, cols = lax.axis_size("row"), lax.axis_size("col")
    k = call(
        lambda k: start_kernel(rows, cols, k), dict(off=offsets), dict(x=x0, h=h),
        dict(local=shape.local, **shape.messages(3, 2)), dict(xs=shape.split, acc=shape.acc),
        dict(flag=(1,), table=offsets.shape),
    )
    near0 = exchange(k)
    return lax.cond(
        k.flag[0] > 0, lambda *a: steps(True, *a), lambda *a: steps(False, *a),
        density, hamiltonian, k.table, branch, k.local, near0,
    )


def solution(mesh):
    return jax.shard_map(
        local,
        mesh=mesh,
        in_specs=(
            P("row", "col", None, None, None, None),
            P("row", "col", None, None, None, None),
            P(),
            P(),
        ),
        out_specs=(
            P("row", "col", None, None, None, None),
            P("row", "col", None, None, None, None),
            P(),
        ),
        check_vma=False,
    )
```

```python
import types

import jax
import jax.numpy as jnp
from jax import lax
from jax.experimental import pallas as pl
from jax.experimental.pallas import tpu as pltpu
from jax.sharding import PartitionSpec as P

F32 = jnp.float32
BF16 = jnp.bfloat16
EXTRA = 8
SIDES = ("row_far", "col_far", "col_near", "row_near")


def each(count, body, rolled):
    if not rolled:
        for i in range(count):
            body(i)
        return

    def step(i, carry):
        body(i)
        return carry

    lax.fori_loop(0, count, step, 0, unroll=2)


def total_of(count, term, first, rolled):
    if not rolled:
        for i in range(count):
            first = first + term(i)
        return first
    return lax.fori_loop(0, count, lambda i, sum_: sum_ + term(i), first)


def iotas(size):
    shape = (size, size)
    return lax.broadcasted_iota(jnp.int32, shape, 0), lax.broadcasted_iota(jnp.int32, shape, 1)


def store_split(dst, index, value):
    size = value.shape[-1]
    high = value.astype(BF16)
    dst[index + (slice(None), slice(0, size))] = high
    dst[index + (slice(None), slice(size, 2 * size))] = (value - high.astype(F32)).astype(BF16)


def split_all(src, dst, rolled):
    layers = src.shape[1]

    def one(i):
        t, s = i // layers, i % layers
        store_split(dst, (t, s), src[t, s])

    each(src.shape[0] * layers, one, rolled)


def quadrants(q):
    size = q.shape[-1] // 2
    return (q[:size, :size] + q[size:, size:]) + (q[:size, size:] + q[size:, :size])


def edge_product(lefts, rights):
    size = lefts[0].shape[0]
    high = [x[:, :size] for x in lefts]
    low = [x[:, size:] for x in lefts]
    lhs = jnp.concatenate([jnp.concatenate(high, 1), jnp.concatenate(low, 1)], 0)
    rhs = jnp.concatenate(rights, 0)
    return quadrants(jnp.dot(lhs, rhs, preferred_element_type=F32))


def turned(value):
    size = value.shape[0]
    parts = [value[:, :size], value[:, size:]]
    return jnp.concatenate([x.astype(F32).T.astype(BF16) for x in parts], 1)


def symmetric(value):
    return value + value.T


def pack_pair(first, second):
    size = first.shape[-1]
    row, col = iotas(size)
    body = jnp.where(row <= col, first, second)
    diagonal = jnp.sum(jnp.where(row == col, second, 0.0), axis=0, keepdims=True)
    return jnp.concatenate([body, jnp.broadcast_to(diagonal, (EXTRA, size))], axis=0)


def unpack_pair(packed):
    size = packed.shape[-1]
    row, col = iotas(size)
    body = packed[:size]
    other = body.T
    second_diagonal = packed[size : size + 1]
    first = jnp.where(row <= col, body, other)
    second = jnp.where(row > col, body, jnp.where(row == col, second_diagonal, other))
    return first, second


def put_pairs(ref, which, blocks):
    for k in range(len(blocks) // 2):
        ref[which, k] = pack_pair(blocks[2 * k], blocks[2 * k + 1])


def put_row(refs, value):
    size = value.shape[-1]
    for ref in refs:
        ref[0, 0, size + 1 : size + 2, :] = value


def get_row(ref):
    size = ref.shape[-1]
    return ref[0, 0, size + 1 : size + 2, :]


def odd(axis):
    return lax.rem(lax.axis_index(axis), 2)


def wrap(layer, layers):
    return lax.rem(layer + 2 * layers, layers)


def slot_offsets(off, t, layers):
    return off[t, 0], off[t, 1], lax.rem(off[t, 2] + layers, layers)


def zero_slot(off, slots):
    z = jnp.int32(0)
    for t in range(slots):
        hit = (off[t, 0] == 0) & (off[t, 1] == 0) & (off[t, 2] == 0)
        z = jnp.where(hit, jnp.int32(t), z)
    return z


def sign_of(branch, k):
    return (2 * branch[k] - 1).astype(F32)


def closes(off, slots, layers, rows, cols):
    def code(r, c, l):
        return (r + 1) * (3 * layers) + (c + 1) * layers + l

    held = jnp.int32(0)
    places = []
    for t in range(slots):
        r, c, l = slot_offsets(off, t, layers)
        nonzero = (r != 0) | (c != 0) | (l != 0)
        held = held | jnp.where(nonzero, jnp.left_shift(jnp.int32(1), code(r, c, l)), 0)
        places.append((r, c, l, nonzero))
    found = jnp.int32(0)
    for i in range(slots):
        for j in range(i + 1):
            (r, c, l, some), (r2, c2, l2, some2) = places[i], places[j]
            r3 = lax.rem(r + r2 + 1 + rows, rows) - 1
            c3 = lax.rem(c + c2 + 1 + cols, cols) - 1
            l3 = lax.rem(l + l2, layers)
            inside = (r3 <= 1) & (c3 <= 1) & some & some2
            place = jnp.where(inside, code(r3, c3, l3), 0)
            hit = jnp.right_shift(held, place) & 1
            found = found | jnp.where(inside, hit, 0)
    return found


def triangle(off, slots, layers):
    def find(test):
        place = jnp.int32(0)
        for t in range(slots):
            place = jnp.where(test(off[t, 0], off[t, 1]), jnp.int32(t), place)
        return place

    g = types.SimpleNamespace()
    g.a = [find(lambda r, c, d=d: (r == d) & (c == 0)) for d in (-1, 1)]
    g.c = [find(lambda r, c, d=d: (r == d) & (c != 0)) for d in (-1, 1)]
    g.beta = off[g.c[1], 1]
    g.b = [find(lambda r, c, d=d: (r == 0) & (c == d * g.beta)) for d in (-1, 1)]
    g.la, g.lb, g.lc = (lax.rem(off[x[1], 2] + layers, layers) for x in (g.a, g.b, g.c))
    return g


def pick(pair, index):
    return jnp.where(index > 0, pair[1], pair[0])


def vertex_sums(off, left, right, acc, rolled):
    slots, layers = left.shape[0], left.shape[1]
    acc[...] = jnp.zeros_like(acc)

    def add(i):
        t, s = i // layers, i % layers
        r, _, l = slot_offsets(off, t, layers)
        q = lax.dot_general(
            left[t, s], right[t, s], (((0,), (0,)), ((), ())), preferred_element_type=F32
        )
        acc[r + 1, lax.rem(s + l, layers)] += quadrants(q)

    each(slots * layers, add, rolled)


def send_sums(acc, which, near, far, sym):
    layers = acc.shape[1]
    parity = odd("row")
    for r, ref in ((2 - 2 * parity, near), (2 * parity, far)):
        blocks = [acc[r, s] for s in range(layers)]
        put_pairs(ref, which, [symmetric(b) for b in blocks] if sym else blocks)


def add_sums(value, near, far, which):
    out = list(value)
    for k in range(len(out) // 2):
        for message in (near, far):
            first, second = unpack_pair(message[which, k])
            out[2 * k] = out[2 * k] + first
            out[2 * k + 1] = out[2 * k + 1] + second
    return out


def fill_neighbours(dst, own, near, far, parity, blocks):
    for k in range(dst.shape[1] // 2):
        for slot, message in ((2 - 2 * parity, near), (2 * parity, far)):
            first, second = blocks(message, k)
            store_split(dst, (slot, 2 * k), first)
            store_split(dst, (slot, 2 * k + 1), second)
    for s in range(dst.shape[1]):
        store_split(dst, (1, s), own[s])


def diagonal_blocks(k, name, own, rows, cols, which):
    def blocks(message, pair):
        return unpack_pair(message[which, pair])

    side = messages(k, name)
    fill_neighbours(rows, own, side["row_near"], side["row_far"], odd("row"), blocks)
    fill_neighbours(cols, own, side["col_near"], side["col_far"], odd("col"), blocks)


def messages(k, name):
    return {side: getattr(k, name + "_" + side) for side in SIDES}


def closed_send(k, out, f32, left, right, cross, sums_at, edges_at):
    slots, layers = left.shape[0], left.shape[1]
    g = triangle(k.off, slots, layers)
    side = messages(k, out)

    def two(x, y):
        lefts, rights = x(left), y(right)
        if not cross:
            return edge_product([lefts], [rights])
        return edge_product([lefts, x(right)], [rights, y(left)])

    parity = odd("row")
    for index, ref in ((1 - parity, side["row_near"]), (parity, side["row_far"])):
        d = 2 * index - 1
        b, c, other = pick(g.b, index), pick(g.c, index), pick(g.b, 1 - index)

        def row_blocks(s, ref=ref, d=d, b=b, c=c, other=other):
            m = wrap(s - d * g.lc, layers)
            if sums_at is not None:
                ref[sums_at, s] = two(lambda x: turned(x[c, m]), lambda x: x[b, m])
            if edges_at is not None:
                ref[edges_at, s] = f32[other, s]

        each(layers, row_blocks, True)
    parity = odd("col")
    for d, ref in ((1 - 2 * parity, side["col_near"]), (2 * parity - 1, side["col_far"])):
        sigma = d * g.beta
        index = (sigma + 1) // 2
        a, other, c = pick(g.a, index), pick(g.a, 1 - index), pick(g.c, 1 - index)

        def col_blocks(s, ref=ref, sigma=sigma, a=a, other=other, c=c):
            m = wrap(s + sigma * g.lb, layers)
            if sums_at is not None:
                ref[sums_at, s] = two(lambda x: x[other, s], lambda x: turned(x[c, m]))
            if edges_at is not None:
                ref[edges_at, s] = f32[a, s]

        each(layers, col_blocks, True)


def closed_edges(k, name, near_a, near_b, value):
    layers = near_a.shape[1]
    g = triangle(k.off, k.off.shape[0], layers)
    side = messages(k, name)
    parity = odd("row")
    for index, key in ((1 - parity, "row_near"), (parity, "row_far")):
        each(
            layers,
            lambda s, i=index, key=key: store_split(near_b, (i, s), value(side[key], key, s)),
            True,
        )
    parity = odd("col")
    for d, key in ((1 - 2 * parity, "col_near"), (2 * parity - 1, "col_far")):
        index = (1 - d * g.beta) // 2
        each(
            layers,
            lambda s, i=index, key=key: store_split(near_a, (i, s), value(side[key], key, s)),
            True,
        )


def closed_terms(k, name, terms, value, lefts, rights):
    layers = terms.shape[1]
    g = triangle(k.off, k.off.shape[0], layers)
    side = messages(k, name)
    parity = odd("row")
    for index, key in ((1 - parity, "row_near"), (parity, "row_far")):
        for s in range(layers):
            k.came_a[index, s] = value(side[key], key, s)
    parity = odd("col")
    for d, key in ((1 - 2 * parity, "col_near"), (2 * parity - 1, "col_far")):
        index = (1 - d * g.beta) // 2
        for s in range(layers):
            k.came_b[index, s] = value(side[key], key, s)

    def product(x, y):
        return edge_product([x(*left) for left in lefts], [y(*right) for right in rights])

    def corner(i):
        index, s = i // layers, i % layers
        sigma = 2 * index - 1
        a, b, c = pick(g.a, index), pick(g.b, index), pick(g.c, index)
        back, on, up = (wrap(s + m, layers) for m in (-sigma * g.lb, sigma * g.lb, sigma * g.la))
        terms[a, s] = k.came_a[index, s] + product(
            lambda f, ea, eb: turned(f[b, back]), lambda f, ea, eb: f[c, back]
        )
        terms[b, s] = k.came_b[index, s] + product(
            lambda f, ea, eb: f[c, s], lambda f, ea, eb: turned(f[a, on])
        )
        terms[c, s] = product(lambda f, ea, eb: f[b, s], lambda f, ea, eb: f[a, on]) + product(
            lambda f, ea, eb: ea[index, s], lambda f, ea, eb: eb[index, up]
        )

    each(2 * layers, corner, True)


def start_kernel(rows, cols, k):
    slots, layers = k.x.shape[0], k.x.shape[1]
    z = zero_slot(k.off, slots)
    for t in range(slots):
        for j in range(3):
            k.table[t, j] = k.off[t, j]
    k.flag[0] = closes(k.off, slots, layers, rows, cols)
    split_all(k.x, k.xs, False)
    vertex_sums(k.off, k.xs, k.xs, k.acc, False)
    for ref in (k.near, k.far, k.side):
        put_pairs(ref, 0, [k.x[z, s] for s in range(layers)])
        put_pairs(ref, 1, [k.h[z, s] for s in range(layers)])
    send_sums(k.acc, 2, k.near, k.far, False)
    for s in range(layers):
        k.local[s] = k.acc[1, s]


def closed_start_kernel(k):
    split_all(k.x, k.xs, True)
    closed_send(k, "out", k.x, k.xs, k.xs, False, 0, 1)
    closed_send(k, "out", k.h, k.xs, k.xs, False, None, 2)


def square_step(k, step, sums_at, closed):
    slots, layers = k.x.shape[0], k.x.shape[1]
    s_k = sign_of(k.branch, step)
    z = zero_slot(k.off, slots)
    split_all(k.x, k.xs, closed)
    own = [k.x[z, s] for s in range(layers)]
    diagonal_blocks(k, "m", own, k.x_rows, k.x_cols, 0)
    square = add_sums([k.x_local[s] for s in range(layers)], k.m_row_near, k.m_row_far, sums_at)
    for s in range(layers):
        k.new[z, s] = own[s] + s_k * (own[s] - square[s])
    if closed:
        closed_edges(k, "e", k.x_near_a, k.x_near_b, lambda ref, key, s: ref[1, s])
        operand = [(k.xs, k.x_near_a, k.x_near_b)]
        closed_terms(k, "e", k.terms, lambda ref, key, s: ref[0, s], operand, operand)

    def edge(i):
        i, s = i // layers, i % layers
        t = i + (i >= z).astype(jnp.int32)
        r, c, l = slot_offsets(k.off, t, layers)
        e = k.xs[t, s]
        product = edge_product([k.x_cols[1 - c, s], e], [e, k.x_rows[1 + r, lax.rem(s + l, layers)]])
        if closed:
            product = product + k.terms[t, s]
        e32 = k.x[t, s]
        k.new[t, s] = e32 + s_k * (e32 - product)

    each((slots - 1) * layers, edge, closed)
    return z


def square_kernel(step, sums_at, closed, k):
    layers = k.x.shape[1]
    z = square_step(k, step, sums_at, closed)
    for ref in (k.near, k.far, k.side):
        put_pairs(ref, 0, [k.new[z, s] for s in range(layers)])
    split_all(k.new, k.ns, closed)
    vertex_sums(k.off, k.ns, k.ns, k.acc, closed)
    send_sums(k.acc, 1, k.near, k.far, False)
    for s in range(layers):
        k.local[s] = k.acc[1, s]
    if closed:
        closed_send(k, "out", k.new, k.ns, k.ns, False, 0, 1)


def turn_square_kernel(step, sums_at, closed, k):
    square_kernel(step, sums_at, closed, k)
    slots, layers, size = k.x.shape[0], k.x.shape[1], k.x.shape[2]
    z = zero_slot(k.off, slots)
    split_all(k.h, k.hs, closed)
    vertex_sums(k.off, k.hs, k.ns, k.acc_h, closed)
    send_sums(k.acc_h, 2, k.near, k.far, True)
    for s in range(layers):
        k.h_local[s] = symmetric(k.acc_h[1, s])
    if closed:
        closed_send(k, "out", None, k.hs, k.ns, True, 2, None)
        closed_send(k, "out", None, k.ns, k.xs, True, 3, None)
    s_next = sign_of(k.branch, step + 1)
    row, col = iotas(size)
    squares = total_of(
        slots * layers,
        lambda i: k.new[i // layers, i % layers] * k.new[i // layers, i % layers],
        jnp.zeros((size, size), F32),
        closed,
    )
    trace = jnp.zeros_like(squares)
    for s in range(layers):
        trace = trace + jnp.where(row == col, k.new[z, s], 0.0)
    part = (1.0 + s_next) * trace - s_next * squares
    k.sums[...] = jnp.broadcast_to(jnp.sum(part, keepdims=True), k.sums.shape)
    put_row((k.near, k.far, k.side), k.sums[0:1, :])


def cross_kernel(closed, k):
    split_all(k.x, k.xs, closed)
    split_all(k.before, k.bs, closed)
    vertex_sums(k.off, k.xs, k.bs, k.acc, closed)
    send_sums(k.acc, 0, k.near, k.far, True)
    for s in range(k.x.shape[1]):
        k.local[s] = symmetric(k.acc[1, s])


def last_square_kernel(step, sums_at, closed, k):
    square_step(k, step, sums_at, closed)
    k.done[...] = jnp.zeros_like(k.done)


def gradient_edges(k, s_k, g, z, closed):
    slots, layers = g.shape[0], g.shape[1]

    def edge(i):
        i, s = i // layers, i % layers
        t = i + (i >= z).astype(jnp.int32)
        r, c, l = slot_offsets(k.off, t, layers)
        e, f = k.gs[t, s], k.xs[t, s]
        b = lax.rem(s + l, layers)
        product = edge_product(
            [k.g_cols[1 - c, s], k.x_cols[1 - c, s], e, f],
            [f, e, k.x_rows[1 + r, b], k.g_rows[1 + r, b]],
        )
        if closed:
            product = product + k.terms[t, s]
        k.new[t, s] = (1.0 + s_k) * g[t, s] - s_k * product

    each((slots - 1) * layers, edge, closed)


def gradient_terms(k, name, value):
    lefts = [(k.gs, k.g_near_a, k.g_near_b), (k.xs, k.x_near_a, k.x_near_b)]
    closed_terms(k, name, k.terms, value, lefts, lefts[::-1])


def gradient_tail(k, z, closed):
    layers = k.x.shape[1]
    for ref in (k.near, k.far, k.side):
        put_pairs(ref, 0, [k.new[z, s] for s in range(layers)])
    split_all(k.new, k.ns, closed)
    split_all(k.before, k.bs, closed)
    vertex_sums(k.off, k.ns, k.bs, k.acc, closed)
    send_sums(k.acc, 1, k.near, k.far, True)
    for s in range(layers):
        k.local[s] = symmetric(k.acc[1, s])
    if closed:
        closed_send(k, "out", k.new, k.ns, k.bs, True, 0, 1)


def first_gradient_kernel(step, closed, k):
    layers = k.x.shape[1]
    s_k = sign_of(k.branch, step)
    z = zero_slot(k.off, k.x.shape[0])
    split_all(k.h, k.gs, closed)
    split_all(k.x, k.xs, closed)
    own_h = [k.h[z, s] for s in range(layers)]
    diagonal_blocks(k, "h", own_h, k.g_rows, k.g_cols, 1)
    diagonal_blocks(k, "m", [k.x[z, s] for s in range(layers)], k.x_rows, k.x_cols, 0)
    cross = add_sums([k.h_local[s] for s in range(layers)], k.m_row_near, k.m_row_far, 2)
    for s in range(layers):
        k.new[z, s] = (1.0 + s_k) * own_h[s] - s_k * cross[s]
    if closed:
        closed_edges(k, "he", k.g_near_a, k.g_near_b, lambda ref, key, s: ref[2, s])
        closed_edges(k, "e", k.x_near_a, k.x_near_b, lambda ref, key, s: ref[1, s])
        gradient_terms(k, "e", lambda ref, key, s: ref[2, s])
    gradient_edges(k, s_k, k.h, z, closed)
    gradient_tail(k, z, closed)

    def weigh(i):
        t, s = i // layers, i % layers
        return ((1.0 + s_k) * k.h[t, s] + k.new[t, s]) * k.x[t, s]

    energy = total_of(k.x.shape[0] * layers, weigh, jnp.zeros_like(k.x[0, 0]), closed)
    k.energy[...] = jnp.broadcast_to(0.5 * jnp.sum(energy, keepdims=True), k.energy.shape)
    for ref, cross in ((k.near, k.cross_near), (k.far, k.cross_far)):
        for pair in range(layers // 2):
            ref[2, pair] = cross[0, pair]


def next_gradient_kernel(step, order, closed, k):
    slots, layers, size = k.x.shape[0], k.x.shape[1], k.x.shape[2]
    s_k = sign_of(k.branch, step)
    s_after = sign_of(k.branch, step + 1)
    sums = k.sums[...] + k.done[...]
    excess = sums[0:1, :] * (1.0 / order) - 0.5
    z = zero_slot(k.off, slots)
    row, col = iotas(size)
    eye = jnp.where(row == col, excess * (1.0 + s_after), 0.0)
    scale = excess * (-2.0 * s_after)

    def assemble(i):
        t, s = i // layers, i % layers
        k.g[t, s] = k.gh[t, s] + scale * k.after[t, s]

    each(slots * layers, assemble, closed)
    for s in range(layers):
        k.g[z, s] = k.g[z, s] + eye
    split_all(k.g, k.gs, closed)
    split_all(k.x, k.xs, closed)
    own_g = [k.g[z, s] for s in range(layers)]
    own_x = [k.x[z, s] for s in range(layers)]

    def blocks(message, pair):
        now, then = (unpack_pair(m[0, pair]) for m in message)
        return [a + scale * b + eye for a, b in zip(now, then)]

    gm, am = messages(k, "gm"), messages(k, "am")
    both = {side: (gm[side], am[side]) for side in SIDES}
    fill_neighbours(k.g_rows, own_g, both["row_near"], both["row_far"], odd("row"), blocks)
    fill_neighbours(k.g_cols, own_g, both["col_near"], both["col_far"], odd("col"), blocks)
    diagonal_blocks(k, "m", own_x, k.x_rows, k.x_cols, 0)
    own_sums = add_sums([k.g_local[s] for s in range(layers)], k.gm_row_near, k.gm_row_far, 1)
    cross_sums = add_sums([k.cross_local[s] for s in range(layers)], k.gm_row_near, k.gm_row_far, 2)
    twice = 2.0 * (1.0 + s_after) * excess
    for s in range(layers):
        cross = own_sums[s] + scale * cross_sums[s] + twice * own_x[s]
        k.new[z, s] = (1.0 + s_k) * own_g[s] - s_k * cross
    if closed:
        ae = messages(k, "ae")
        closed_edges(
            k, "ge", k.g_near_a, k.g_near_b, lambda ref, key, s: ref[1, s] + scale * ae[key][1, s]
        )
        closed_edges(k, "e", k.x_near_a, k.x_near_b, lambda ref, key, s: ref[1, s])
        gradient_terms(k, "ge", lambda ref, key, s: ref[0, s] + scale * ae[key][3, s])
    gradient_edges(k, s_k, k.g, z, closed)
    gradient_tail(k, z, closed)
    k.energy[...] = jnp.broadcast_to(sums[1:2, :], k.energy.shape)
    put_row((k.near, k.far, k.side), sums[1:2, :])


def last_gradient_kernel(step, closed, k):
    layers = k.x.shape[1]
    s_k = sign_of(k.branch, step)
    z = zero_slot(k.off, k.x.shape[0])
    split_all(k.g, k.gs, closed)
    split_all(k.x, k.xs, closed)
    own_g = [k.g[z, s] for s in range(layers)]
    diagonal_blocks(k, "gm", own_g, k.g_rows, k.g_cols, 0)
    diagonal_blocks(k, "m", [k.x[z, s] for s in range(layers)], k.x_rows, k.x_cols, 0)
    cross = add_sums([k.g_local[s] for s in range(layers)], k.gm_row_near, k.gm_row_far, 1)
    for s in range(layers):
        k.new[z, s] = (1.0 + s_k) * own_g[s] - s_k * cross[s]
    if closed:
        closed_edges(k, "ge", k.g_near_a, k.g_near_b, lambda ref, key, s: ref[1, s])
        closed_edges(k, "e", k.x_near_a, k.x_near_b, lambda ref, key, s: ref[1, s])
        gradient_terms(k, "ge", lambda ref, key, s: ref[0, s])
    gradient_edges(k, s_k, k.g, z, closed)


def call(kernel, smem, vmem, outs, scratch, smem_outs=()):
    names = [*smem, *vmem, *outs, *dict(smem_outs), *scratch]
    small = dict(smem_outs)

    def body(*refs):
        kernel(types.SimpleNamespace(**dict(zip(names, refs))))

    results = pl.pallas_call(
        body,
        out_shape=[jax.ShapeDtypeStruct(shape, F32) for shape in outs.values()]
        + [jax.ShapeDtypeStruct(shape, jnp.int32) for shape in small.values()],
        in_specs=[pl.BlockSpec(memory_space=pltpu.SMEM)] * len(smem)
        + [pl.BlockSpec(memory_space=pltpu.VMEM)] * len(vmem),
        out_specs=[pl.BlockSpec(memory_space=pltpu.VMEM)] * len(outs)
        + [pl.BlockSpec(memory_space=pltpu.SMEM)] * len(small),
        scratch_shapes=list(scratch.values()),
        compiler_params=pltpu.CompilerParams(vmem_limit_bytes=40 * 1024 * 1024),
        cost_estimate=pl.CostEstimate(flops=2_000_000_000, bytes_accessed=6_000_000, transcendentals=0),
    )(*smem.values(), *vmem.values())
    return types.SimpleNamespace(**dict(zip([*outs, *small], results)))


def pairs_of(axis):
    count = lax.axis_size(axis)
    near = [(i, i ^ 1) for i in range(count)]
    far = [(i, (i - 1) % count if i % 2 == 0 else (i + 1) % count) for i in range(count)]
    return near, far


def swap(col_far, col_near, row_near, row_far):
    near_row, far_row = pairs_of("row")
    near_col, far_col = pairs_of("col")
    return dict(
        col_far=lax.ppermute(col_far, "col", far_col),
        col_near=lax.ppermute(col_near, "col", near_col),
        row_near=lax.ppermute(row_near, "row", near_row),
        row_far=lax.ppermute(row_far, "row", far_row),
    )


def exchange(k):
    out = swap(k.side, k.side, k.near, k.far)
    out["first"] = out["row_far"][0, 0, -EXTRA:, :] + out["col_far"][0, 0, -EXTRA:, :]
    return out


def exchange_edges(k):
    return swap(k.out_col_far, k.out_col_near, k.out_row_near, k.out_row_far)


def named(name, arrays):
    return {name + "_" + side: arrays[side] for side in SIDES}


def doubling(value, axis, steps):
    for step in steps:
        count = lax.axis_size(axis)
        value = value + lax.ppermute(value, axis, [(i, i ^ step) for i in range(count)])
    return value


def powers(axis):
    count = lax.axis_size(axis)
    return [] if count & (count - 1) else [1 << i for i in range(count.bit_length() - 1)]


def col_first(value):
    steps = powers("col")
    return doubling(value, "col", steps[:1]) if steps else lax.psum(value, "col")


def col_rest(value):
    return doubling(value, "col", powers("col")[1:])


def row_total(value, came):
    if lax.axis_size("row") == 4:
        rest = lax.ppermute(value, "row", [(i, i ^ 2) for i in range(4)])
        row = value.shape[-1] + 1
        near, far = (came[side][0, 0, row : row + 1] for side in ("row_near", "row_far"))
        return (value + near) + (far + rest)
    steps = powers("row")
    return doubling(value, "row", steps) if steps else lax.psum(value, "row")


class Shapes:
    def __init__(self, density):
        slots, layers, size = density.shape[2:5]
        self.full = (slots, layers, size, size)
        self.local = (layers, size, size)
        self.tile = (8, size)
        self.order = float(size * layers * lax.axis_size("row") * lax.axis_size("col"))
        self.split = pltpu.VMEM((slots, layers, size, 2 * size), BF16)
        self.three = pltpu.VMEM((3, layers, size, 2 * size), BF16)
        self.two = pltpu.VMEM((2, layers, size, 2 * size), BF16)
        self.two_wide = pltpu.VMEM((2, layers, size, size), F32)
        self.acc = pltpu.VMEM((3, layers, size, size), F32)
        self.wide = pltpu.VMEM(self.full, F32)
        self.pairs = (layers // 2, size + EXTRA, size)

    def messages(self, rows, cols):
        return dict(near=(rows, *self.pairs), far=(rows, *self.pairs), side=(cols, *self.pairs))

    def edges(self, count, closed):
        return {"out_" + side: (count, *self.local) for side in SIDES} if closed else {}

    def near_edges(self, names, closed):
        if not closed:
            return {}
        out = dict(terms=self.wide, came_a=self.two_wide, came_b=self.two_wide)
        for name in names:
            out[name + "_near_a"] = self.two
            out[name + "_near_b"] = self.two
        return out


def steps(closed, density, hamiltonian, table, branch, local0, near0):
    shape = Shapes(density)
    x0 = density.reshape(shape.full)
    h = hamiltonian.reshape(shape.full)
    full, local, tile, order = shape.full, shape.local, shape.tile, shape.order
    split, three, acc = shape.split, shape.three, shape.acc
    smem = dict(off=table, branch=branch)
    square_scratch = dict(xs=split, x_rows=three, x_cols=three, **shape.near_edges(["x"], closed))
    pair_scratch = dict(
        gs=split, xs=split, g_rows=three, g_cols=three, x_rows=three, x_cols=three,
        **shape.near_edges(["g", "x"], closed),
    )
    tail = dict(ns=split, bs=split, acc=acc)

    def edges(**fields):
        out = {}
        for name, arrays in fields.items():
            out.update(named(name, arrays) if closed else {})
        return out

    edge0 = edge1 = edge2 = edge_gh = edge_g1 = None
    if closed:
        k = call(closed_start_kernel, dict(off=table), dict(x=x0, h=h), shape.edges(3, True), dict(xs=split))
        edge0 = exchange_edges(k)
    k = call(
        lambda k: square_kernel(0, 2, closed, k), smem,
        dict(x=x0, x_local=local0, first=near0["first"], **named("m", near0), **edges(e=edge0)),
        dict(new=full, local=local, **shape.messages(2, 1), **shape.edges(2, closed)),
        dict(ns=split, acc=acc, **square_scratch),
    )
    x1, local1, near1 = k.new, k.local, exchange(k)
    if closed:
        edge1 = exchange_edges(k)
    k = call(
        lambda k: turn_square_kernel(1, 1, closed, k), smem,
        dict(x=x1, x_local=local1, h=h, first=near1["first"], **named("m", near1), **edges(e=edge1)),
        dict(new=full, local=local, h_local=local, sums=tile,
             **shape.messages(3, 1), **shape.edges(4, closed)),
        dict(ns=split, hs=split, acc=acc, acc_h=acc, **square_scratch),
    )
    x2, local2, h_local, occupied, near2 = k.new, k.local, k.h_local, k.sums, exchange(k)
    if closed:
        edge2 = exchange_edges(k)
    cross = call(
        lambda k: cross_kernel(closed, k), dict(off=table), dict(x=x2, before=x1),
        dict(near=(1, *shape.pairs), far=(1, *shape.pairs), local=local), dict(xs=split, bs=split, acc=acc),
    )
    occupied = col_first(row_total(occupied, near2))
    k = call(
        lambda k: first_gradient_kernel(2, closed, k), smem,
        dict(h=h, x=x2, before=x1, h_local=h_local, first=near2["first"],
             cross_near=cross.near, cross_far=cross.far, **named("h", near0), **named("m", near2),
             **edges(he=edge0, e=edge2)),
        dict(new=full, local=local, energy=tile, **shape.messages(3, 1), **shape.edges(2, closed)),
        dict(**pair_scratch, **tail),
    )
    gh, gh_local, energy, near_gh = k.new, k.local, k.energy, exchange(k)
    if closed:
        edge_gh = exchange_edges(k)
    row = lax.broadcasted_iota(jnp.int32, tile, 0)
    sums = col_rest(jnp.where(row == 0, occupied, energy))
    k = call(
        lambda k: last_square_kernel(2, 1, closed, k), smem,
        dict(**named("m", near2), x=x2, x_local=local2, **edges(e=edge2)),
        dict(new=full, done=tile), square_scratch,
    )
    x3, done = k.new, k.done
    k = call(
        lambda k: next_gradient_kernel(1, order, closed, k), smem,
        dict(sums=sums, done=done, first=near_gh["first"], gh=gh, after=x2, x=x1, before=x0, g_local=gh_local,
             cross_local=cross.local, **named("gm", near_gh), **named("am", near2), **named("m", near1),
             **edges(ge=edge_gh, ae=edge2, e=edge1)),
        dict(new=full, local=local, energy=tile,
             **shape.messages(2, 1), **shape.edges(2, closed)),
        dict(g=shape.wide, **pair_scratch, **tail),
    )
    g1, g1_local, energy, near_g1 = k.new, k.local, k.energy, exchange(k)
    if closed:
        edge_g1 = exchange_edges(k)
    energy = col_first(row_total(energy, near_g1))
    k = call(
        lambda k: last_gradient_kernel(0, closed, k), smem,
        dict(g=g1, x=x0, g_local=g1_local, first=near_g1["first"], **named("gm", near_g1), **named("m", near0),
             **edges(ge=edge_g1, e=edge0)),
        dict(new=full), pair_scratch,
    )
    lane = lax.broadcasted_iota(jnp.int32, (2,), 0)
    totals = jnp.where(lane == 0, energy[0, :2], sums[0, :2]) / order
    return x3.reshape(density.shape), k.new.reshape(density.shape), totals


def local(density, hamiltonian, offsets, branch):
    shape = Shapes(density)
    x0 = density.reshape(shape.full)
    h = hamiltonian.reshape(shape.full)
    rows, cols = lax.axis_size("row"), lax.axis_size("col")
    k = call(
        lambda k: start_kernel(rows, cols, k), dict(off=offsets), dict(x=x0, h=h),
        dict(local=shape.local, **shape.messages(3, 2)), dict(xs=shape.split, acc=shape.acc),
        dict(flag=(1,), table=offsets.shape),
    )
    near0 = exchange(k)
    return lax.cond(
        k.flag[0] > 0, lambda *a: steps(True, *a), lambda *a: steps(False, *a),
        density, hamiltonian, k.table, branch, k.local, near0,
    )


def solution(mesh):
    return jax.shard_map(
        local,
        mesh=mesh,
        in_specs=(
            P("row", "col", None, None, None, None),
            P("row", "col", None, None, None, None),
            P(),
            P(),
        ),
        out_specs=(
            P("row", "col", None, None, None, None),
            P("row", "col", None, None, None, None),
            P(),
        ),
        check_vma=False,
    )
```
